1024 devices in a mesh: tiles: 128 (over x, z, core), sub: 8 (over y).
Axes of the slice: x: 8, y: 8, z: 8, core: 2. Of those that a mesh axis runs over, the one named last changes fastest.
Arguments:
- state: float32 [1024, 4, 2, 3600], P(('tiles', 'sub')), may hold values from -6 to 6
- surface: float32 [1024, 3600], P(('tiles', 'sub')), may hold values from -6 to 6
- land_mask: int32 [1024, 3600], P(('tiles', 'sub')), may hold values 0 or 1
- neighbours: int32 [1024, 4], P(('tiles', 'sub')), may hold values from -1 to 1023, as said below
Outputs:
- new_state: float32 [1024, 4, 2, 3600], P(('tiles', 'sub'))
- new_surface: float32 [1024, 3600], P(('tiles', 'sub'))
The draws below stay inside these ranges and needn't reach their ends.
Inputs may be any that keep to these rules, and one draw needn't show every extreme that they name: Every listed tile g satisfies g // 8 differing from the tile's own index // 8 by at most 1; tiles are ocean tiles of a grid of 128 columns, each of 8 ocean tiles in some order, and the lists are those of that grid: north and south neighbours lie in the tile's own column, an east neighbour in the next column, a west neighbour in the previous column.
All inputs are finite; a program needn't handle non-finite values. No bound on the sum of `land_mask` on one device may be relied on, other than what follows from the above.
Results may differ from the reference program's by a relative error of at most 0.0001.
Values sent between devices are 32-bit elements; how exact they have to be, the bound alone decides.
A program may use at most 32 MiB of HBM per device.

```python
import jax
import jax.numpy as jnp
from jax import lax

TILE = 60
LEV = 2
TPD = 1
STEPS = 2
SUBCYCLES = 4
NT = 1024
N_TILES = 128
N_SUB = 8


def draw_neighbours(key, part):
    slots = TPD * N_SUB
    rows = 2 * slots
    keys = jax.random.split(key, N_TILES)
    orders = jax.vmap(lambda single: jax.random.permutation(single, rows))(keys)
    ocean_rows = orders[:, :slots]
    ranks = jnp.argsort(orders, axis=1)
    slot_of = jnp.where(ranks < slots, ranks, -1)
    padded = jnp.pad(slot_of, 1, constant_values=-1)
    column = jnp.arange(N_TILES)[:, None] + jnp.zeros((1, slots), jnp.int32)
    north = padded[column + 1, ocean_rows]
    south = padded[column + 1, ocean_rows + 2]
    west = padded[column, ocean_rows + 1]
    east = padded[column + 2, ocean_rows + 1]
    north_id = jnp.where(north >= 0, column * slots + north, -1)
    south_id = jnp.where(south >= 0, column * slots + south, -1)
    west_id = jnp.where(west >= 0, (column - 1) * slots + west, -1)
    east_id = jnp.where(east >= 0, (column + 1) * slots + east, -1)
    stacked = jnp.stack([north_id, east_id, south_id, west_id], axis=-1)
    return stacked.reshape(N_TILES * slots, 4).astype(jnp.int32)


def set_ends(drawn, key, least, largest):
    spot = [jax.random.randint(jax.random.fold_in(key, axis), (), 0, length) for axis, length in enumerate(drawn.shape)]
    main_axis = drawn.shape.index(max(drawn.shape))
    beside = spot[:main_axis] + [(spot[main_axis] + 1) % drawn.shape[main_axis]] + spot[main_axis + 1:]
    return drawn.at[tuple(spot)].set(least).at[tuple(beside)].set(largest)


def shard_levels(own_key, extent, shards, low, largest):
    def one(axis_at, shards_of):
        draws = jax.random.uniform(jax.random.fold_in(jax.random.fold_in(own_key, 6), axis_at), (shards_of,), jnp.float32, low / len(shards), largest / len(shards))
        return jnp.repeat(jnp.exp(draws), extent[axis_at] // shards_of).reshape((-1,) + (1,) * (len(extent) - axis_at - 1))

    loudness = one(*shards[0])
    for cut in shards[1:]:
        loudness = loudness * one(*cut)
    return loudness


def scatter_about(key, extent, scale, limit, shards=(), kind=jnp.bfloat16):
    entries = scale * jax.random.normal(key, extent, jnp.float32)
    if shards:
        entries = entries * shard_levels(key, extent, shards, -0.22, 0.18)
    return jnp.clip(entries, -limit, limit).astype(kind)


def setup_inputs(seed: int = 0) -> dict:
    splits = jax.random.split(jax.random.key(seed), 5)
    return {
        "state": scatter_about(splits[0], (NT, 4, LEV, TILE * TILE), 1.0, 6.0, ((0, 1024),), jnp.float32),
        "surface": scatter_about(splits[1], (NT, TILE * TILE), 1.0, 6.0, ((0, 1024),), jnp.float32),
        "land_mask": set_ends((jax.random.randint(splits[2], (NT, TILE * TILE), 0, 5) < 4).astype(jnp.int32), jax.random.fold_in(splits[2], 1), 0, 1),
        "neighbours": draw_neighbours(jax.random.fold_in(splits[4], 71), 0),
    }


time_step = 0.2
mixing = 0.02
coriolis = 0.5
gravity_step = 0.25
depth_step = 0.25


def edge_panels(field):
    north = field[..., 0:2, :]
    south = field[..., ::-1, :][..., 0:2, :]
    west = jnp.swapaxes(field[..., :, 0:2], -1, -2)
    east = jnp.swapaxes(field[..., :, ::-1][..., :, 0:2], -1, -2)
    stacked = jnp.stack([north, east, south, west], axis=-3)
    return stacked.reshape(field.shape[:-2] + (8 * TILE,))


def pick(candidates, index, valid):
    result = []
    for direction in range(4):
        rows = jnp.take(candidates, index[:, direction], axis=0)
        rows = rows.reshape(rows.shape[:-1] + (4, 2, TILE))[..., (direction + 2) % 4, :, :]
        keep = valid[:, direction].reshape((-1,) + (1,) * (rows.ndim - 1))
        result.append(jnp.where(keep, rows, jnp.zeros_like(rows)))
    return result


def extend(field, north, east, south, west):
    corner = jnp.zeros(field.shape[:-2] + (2, 2), field.dtype)
    top = jnp.concatenate([corner, north[..., ::-1, :], corner], -1)
    bottom = jnp.concatenate([corner, south, corner], -1)
    left = jnp.swapaxes(west[..., ::-1, :], -1, -2)
    right = jnp.swapaxes(east, -1, -2)
    middle = jnp.concatenate([left, field, right], -1)
    return jnp.concatenate([top, middle, bottom], -2)


def laplace(field):
    widths = [(0, 0)] * (field.ndim - 2) + [(1, 1), (1, 1)]
    padded = jnp.pad(field, widths)
    return padded[..., 2:, 1:-1] + padded[..., :-2, 1:-1] + padded[..., 1:-1, 2:] + padded[..., 1:-1, :-2] - 4.0 * field


def clinic(fields, extended, wet):
    last = TILE + 2
    grad_x = (extended[..., 2:last, 3:last + 1] - extended[..., 2:last, 1:last - 1]) * 0.5
    grad_y = (extended[..., 3:last + 1, 2:last] - extended[..., 1:last - 1, 2:last]) * 0.5
    smooth = laplace(laplace(extended))[..., 2:last, 2:last]
    zonal = fields[..., 2, :, :, :]
    meridional = fields[..., 3, :, :, :]
    tend = -(zonal * grad_x + meridional * grad_y) - mixing * smooth
    nothing = jnp.zeros_like(zonal)
    turning = jnp.stack([nothing, nothing, coriolis * meridional, -coriolis * zonal], axis=-4)
    return (fields + time_step * (tend + turning)) * wet


def depth_sum(field):
    levels = field.shape[-3]
    weights = 2.0 * (jnp.arange(levels).astype(jnp.float32) + 1.0) / (levels * (levels + 1))
    return jnp.sum(field * weights[:, None, None], axis=-3)


def tropic(height, zonal, meridional, wet):
    full = TILE + 4
    grad_x = (height[..., 1:full - 1, 2:full] - height[..., 1:full - 1, 0:full - 2]) * 0.5
    grad_y = (height[..., 2:full, 1:full - 1] - height[..., 0:full - 2, 1:full - 1]) * 0.5
    new_u = zonal[..., 1:full - 1, 1:full - 1] - gravity_step * grad_x
    new_v = meridional[..., 1:full - 1, 1:full - 1] - gravity_step * grad_y
    last = TILE + 1
    spread = (new_u[..., 1:last, 2:last + 1] - new_u[..., 1:last, 0:last - 1]
              + new_v[..., 2:last + 1, 1:last] - new_v[..., 0:last - 1, 1:last]) * 0.5
    height_new = (height[..., 2:last + 1, 2:last + 1] - depth_step * spread) * wet
    return height_new, new_u[..., 1:last, 1:last] * wet, new_v[..., 1:last, 1:last] * wet


def couple(fields, change_u, change_v):
    zonal = fields[:, 2] + change_u[:, None]
    meridional = fields[:, 3] + change_v[:, None]
    return jnp.concatenate([fields[:, 0:2], zonal[:, None], meridional[:, None]], axis=1)


def reference(state, surface, land_mask, neighbours):
    count = state.shape[0]
    levels = state.shape[2]
    wet = land_mask.reshape(count, TILE, TILE).astype(jnp.float32)
    fields = state.reshape(count, 4, levels, TILE, TILE) * wet[:, None, None]
    height = surface.reshape(count, TILE, TILE) * wet
    valid = neighbours >= 0
    index = jnp.where(valid, neighbours, 0).astype(jnp.int32)
    for step in range(STEPS):
        halos = pick(edge_panels(fields), index, valid)

        def one_tile(items):
            tile_fields, north, east, south, west, tile_wet = items
            extended = extend(tile_fields, north, east, south, west)
            return clinic(tile_fields, extended, tile_wet)

        fields = lax.map(one_tile, (fields, halos[0], halos[1], halos[2], halos[3], wet))
        old_u = depth_sum(fields[:, 2])
        old_v = depth_sum(fields[:, 3])
        zonal, meridional = old_u, old_v
        for cycle in range(SUBCYCLES):
            stacked = jnp.stack([height, zonal, meridional], axis=1)
            near = pick(edge_panels(stacked), index, valid)
            extended = extend(stacked, near[0], near[1], near[2], near[3])
            height, zonal, meridional = tropic(extended[:, 0], extended[:, 1], extended[:, 2], wet)
        fields = couple(fields, zonal - old_u, meridional - old_v)
    return fields.reshape(count, 4, levels, TILE * TILE), height.reshape(count, TILE * TILE)
```

```python
import functools

import jax
import jax.numpy as jnp
from jax import lax
from jax.experimental import pallas as pl
from jax.experimental.pallas import tpu as pltpu
from jax.sharding import PartitionSpec as P

MESH = pl.DeviceIdType.MESH
TILE = 60
STEPS = 2
SUBCYCLES = 4
SUB = 8

time_step = 0.2
mixing = 0.02
coriolis = 0.5
gravity_step = 0.25
depth_step = 0.25

TOP = 24
ROWS = 112
ETA, WET = 8, 9
ITEMS = (
    [(4 + i, 18 * i, 18) for i in range(4)]
    + [(ETA, 72, 16), (WET, 88, 16)]
    + [(i, 104 + 4 * i, 4) for i in range(4)]
)


def lanes(shape):
    return lax.broadcasted_iota(jnp.int32, shape, len(shape) - 1)


def turn(x, shift):
    shift %= 128
    return pltpu.roll(x, shift, x.ndim - 1) if shift else x


def within(lane, first, count):
    return (lane >= first) & (lane < first + count)


def pack(D, p1):
    def both(item, north, south, count):
        return D[item, TOP + north : TOP + north + count] + turn(D[item, TOP + south : TOP + south + count], 64)

    for i in range(4):
        p1[i, 0:16] = both(4 + i, 0, 42, 16)
        p1[6, 4 * i : 4 * i + 4] = both(i, 0, 56, 4)
        p1[7, 2 * i : 2 * i + 2] = both(4 + i, 16, 58, 2)
    p1[4, 0:16] = both(ETA, 0, 44, 16)
    p1[5, 0:16] = both(WET, 0, 44, 16)
    p1[7, 8:16] = jnp.zeros((8, 128), jnp.float32)
    lane = lanes((64, 128))
    east = west = jnp.zeros((64, 128), jnp.float32)
    for item, first, depth in ITEMS:
        whole = D[item, TOP : TOP + 64]
        here = within(lane, first, depth)
        east = jnp.where(here, turn(whole, first - (TILE - depth)), east)
        west = jnp.where(here, turn(whole, first), west)
    for m in range(SUB):
        p1[m, 16:24] = east[8 * m : 8 * m + 8]
        p1[m, 24:32] = west[8 * m : 8 * m + 8]


def take(table, index):
    out = jnp.full((SUB, 128), -1, jnp.int32)
    for k in range(SUB):
        out = jnp.where(index == k, jnp.broadcast_to(table[k : k + 1], (SUB, 128)), out)
    return out


def wanted(ids, me, lists):
    def side(column, direction):
        return jnp.concatenate([ids[column, r, direction : direction + 1] for r in range(SUB)], 0)

    north, south = side(1, 0), side(1, 2)
    lists[0] = jnp.where(lanes((SUB, 128)) < 64, south, north)
    for at, column, direction in ((1, 2, 3), (3, 0, 1)):
        beside, above, below = side(column, direction), side(column, 0), side(column, 2)
        up = jnp.where(above >= 0, take(beside, above), take(north, beside))
        down = jnp.where(below >= 0, take(beside, below), take(south, beside))
        lists[at] = beside
        lists[at + 1] = jnp.where(me >= 4, up, down)


def unpack(D, rns, re, rw, eb, wb):
    for held, got in ((eb, re), (wb, rw)):
        for j in range(3):
            held[4 + 8 * j : 12 + 8 * j] = got[5 + j, 8:16]
        for m in range(SUB):
            held[TOP + 8 * m : TOP + 8 * m + 8] = got[m, 0:8]
        for j in range(3):
            held[84 + 8 * j : 92 + 8 * j] = got[j, 8:16]

    for item, first, depth in ITEMS:
        begin, count = TOP - depth, TILE + 2 * depth
        lane = lanes((count, 128))
        east = turn(eb[begin : begin + count], TILE - first)
        west = turn(wb[begin : begin + count], 128 - depth - first)
        sides = jnp.where(within(lane, TILE, depth), east, jnp.where(lane >= 128 - depth, west, 0.0))
        D[item, begin : begin + count] = D[item, begin : begin + count] + sides

    def put(item, rows, north, south):
        count = rows.shape[0]
        tile = lanes((count, 128)) < TILE
        D[item, TOP + north : TOP + north + count] += jnp.where(tile, turn(rows, 64), 0.0)
        D[item, TOP + south : TOP + south + count] += jnp.where(tile, rows, 0.0)

    for i in range(4):
        put(4 + i, rns[i], -18, 60)
        put(4 + i, rns[7, 2 * i : 2 * i + 2], -2, 76)
        put(i, rns[6, 4 * i : 4 * i + 4], -4, 60)
    put(ETA, rns[4], -16, 60)
    put(WET, rns[5], -16, 60)


def clinic(D, N, item, begin, count):
    level = item % 2

    def at(which, shift=0):
        return D[which, begin + shift : begin + shift + count]

    mid, north, south = at(item), at(item, -1), at(item, 1)
    wet = at(WET)
    u, v = at(4 + level), at(6 + level)
    right, left = turn(mid, -1), turn(mid, 1)
    cross = 2.0 * (north + south) - 8.0 * mid
    smooth = (
        20.0 * mid
        - 8.0 * (north + south)
        + at(item, -2)
        + at(item, 2)
        + turn(cross + right, -1)
        + turn(cross + left, 1)
    )
    tend = -(u * ((right - left) * 0.5) + v * ((south - north) * 0.5)) - mixing * smooth
    if item // 2 == 2:
        tend = tend + coriolis * v
    if item // 2 == 3:
        tend = tend - coriolis * u
    N[item, begin : begin + count] = (mid + time_step * tend) * wet
    lane = lanes((2, 128))
    for row in (TOP - 1, TOP + TILE - 1):
        swapped = jnp.concatenate([D[item, row + 1 : row + 2], D[item, row : row + 1]], 0)
        diagonal = jnp.where(
            (lane == 0) | (lane == TILE),
            turn(swapped, 1),
            jnp.where((lane == 127) | (lane == TILE - 1), turn(swapped, -1), 0.0),
        )
        N[item, row : row + 2] += (2.0 * time_step * mixing) * diagonal * D[WET, row : row + 2]


def tropic(heights, norths, wet_at, eta, zonal, meridional, begin, count):
    for _ in range(SUBCYCLES):
        heights[begin : begin + count] = eta
        norths[begin : begin + count] = meridional

        def a(shift):
            return heights[begin + shift : begin + shift + count]

        def c(shift):
            return norths[begin + shift : begin + shift + count]

        new_u = zonal - (gravity_step * 0.5) * (turn(eta, -1) - turn(eta, 1))
        new_v = meridional - (gravity_step * 0.5) * (a(1) - a(-1))
        along = (c(1) - c(-1)) - (gravity_step * 0.5) * ((a(2) - eta) - (eta - a(-2)))
        spread = (turn(new_u, -1) - turn(new_u, 1)) + along
        wet = wet_at(begin, count)
        eta = (eta - (depth_step * 0.5) * spread) * wet
        zonal, meridional = new_u * wet, new_v * wet
    return eta, zonal, meridional


def kernel(
    columns,
    near,
    state,
    surface,
    wet,
    new_state,
    new_surface,
    D,
    N,
    heights,
    norths,
    p1,
    c1,
    my_ids,
    ids,
    lists,
    out_own,
    out_up,
    out_down,
    rns,
    re,
    rw,
    eb,
    wb,
    sent,
    came,
):
    column, me = lax.axis_index("tiles"), lax.axis_index("sub")
    after, before = lax.rem(column + 1, columns), lax.rem(column + columns - 1, columns)
    others = [lax.rem(me + k, SUB) for k in range(SUB)]
    own = [(column, r) for r in others[1:]]
    ups = [(after, r) for r in others]
    downs = [(before, r) for r in others]

    barrier = pltpu.get_barrier_semaphore()
    for device in own + ups + downs:
        pl.semaphore_signal(barrier, inc=1, device_id=device, device_id_type=MESH)

    row = lax.broadcasted_iota(jnp.int32, (SUB, 128), 0)
    mine = jnp.full((SUB, 128), -1, jnp.int32)
    for direction, base in enumerate((column, column + 1, column, column - 1)):
        listed = near[0, direction]
        slot = jnp.where(listed >= 0, listed - base * SUB, -1)
        mine = jnp.where(row == direction, slot, mine)
    my_ids[...] = mine
    ids[1, me] = mine

    D[...] = jnp.zeros_like(D)
    ocean = wet[...]
    D[WET, TOP : TOP + TILE, 0:TILE] = ocean
    D[ETA, TOP : TOP + TILE, 0:TILE] = surface[...] * ocean
    for item in range(8):
        D[item, TOP : TOP + TILE, 0:TILE] = state[item] * ocean
    pack(D, p1)
    c1[me] = p1[me]

    def send(source, target, kind, device):
        pltpu.make_async_remote_copy(
            src_ref=source,
            dst_ref=target,
            send_sem=sent.at[kind],
            recv_sem=came.at[kind],
            device_id=device,
            device_id_type=MESH,
        ).start()

    pl.semaphore_wait(barrier, len(own + ups + downs))
    for device in own:
        send(p1.at[device[1]], c1.at[me], 0, device)
    for device in own:
        send(my_ids, ids.at[1, me], 1, device)
    for device in ups:
        send(my_ids, ids.at[0, me], 2, device)
    for device in downs:
        send(my_ids, ids.at[2, me], 3, device)

    def wait(ref, semaphore):
        pltpu.make_async_copy(ref, ref, semaphore).wait()

    seven, eight = pl.ds(0, SUB - 1), pl.ds(0, SUB)
    wait(ids.at[1, seven], came.at[1])
    wait(ids.at[0, eight], came.at[2])
    wait(ids.at[2, eight], came.at[3])
    wanted(ids, me, lists)
    wait(c1.at[seven], came.at[0])

    def picked(which, r, first, count):
        want = jnp.broadcast_to(lists[which, pl.ds(r, 1)], (8, 128))
        outs = [jnp.zeros((8, 128), jnp.float32) for _ in range(count // 8)]
        for k in range(SUB):
            hit = want == k
            for i in range(count // 8):
                outs[i] = jnp.where(hit, c1[k, first + 8 * i : first + 8 * i + 8], outs[i])
        return outs

    for k in range(SUB):
        r = others[k]
        parts = picked(0, r, 0, 16)
        for at in range(2):
            if k:
                out_own[r, 8 * at : 8 * at + 8] = parts[at]
            else:
                rns[me, 8 * at : 8 * at + 8] = parts[at]
        if k:
            send(out_own.at[r], rns.at[me], 4, (column, r))
        out_up[r, 0:8] = picked(1, r, 16, 8)[0]
        out_up[r, 8:16] = picked(2, r, 16, 8)[0]
        send(out_up.at[r], rw.at[me], 5, (after, r))
        out_down[r, 0:8] = picked(3, r, 24, 8)[0]
        out_down[r, 8:16] = picked(4, r, 24, 8)[0]
        send(out_down.at[r], re.at[me], 6, (before, r))

    wait(rns.at[seven], came.at[4])
    wait(rw.at[eight], came.at[5])
    wait(re.at[eight], came.at[6])

    unpack(D, rns, re, rw, eb, wb)
    N[...] = jnp.zeros_like(N)
    heights[...] = jnp.zeros_like(heights)
    norths[...] = jnp.zeros_like(norths)
    weights = (2.0 / 6.0, 4.0 / 6.0)
    fields, other = D, N
    wet_at = lambda begin, count: D[WET, begin : begin + count]
    for step in range(STEPS):
        begin, count = ((8, 96), (16, 80))[step]
        tracer = ((16, 72), (24, 64))[step]
        for item in range(4):
            clinic(fields, other, item, *tracer)
        for item in range(4, 8):
            clinic(fields, other, item, begin, count)
        rows = slice(begin, begin + count)
        old_u = weights[0] * other[4, rows] + weights[1] * other[5, rows]
        old_v = weights[0] * other[6, rows] + weights[1] * other[7, rows]
        eta, zonal, meridional = tropic(heights, norths, wet_at, fields[ETA, rows], old_u, old_v, begin, count)
        other[ETA, rows] = eta
        other[WET] = fields[WET]
        for level in range(2):
            other[4 + level, rows] += zonal - old_u
            other[6 + level, rows] += meridional - old_v
        fields, other = other, fields

    for item in range(8):
        new_state[item] = fields[item, TOP : TOP + TILE, 0:TILE]
    new_surface[...] = fields[ETA, TOP : TOP + TILE, 0:TILE]

    wait(c1.at[seven], sent.at[0])
    wait(ids.at[1, seven], sent.at[1])
    wait(ids.at[0, eight], sent.at[2])
    wait(ids.at[2, eight], sent.at[3])
    wait(rns.at[seven], sent.at[4])
    wait(rw.at[eight], sent.at[5])
    wait(re.at[eight], sent.at[6])


def shards(columns, state, surface, land_mask, neighbours):
    wet = land_mask.reshape(TILE, TILE).astype(jnp.float32)
    vmem = pl.BlockSpec(memory_space=pltpu.VMEM)
    f32 = lambda *shape: pltpu.VMEM(shape, jnp.float32)
    new_state, new_surface = pl.pallas_call(
        functools.partial(kernel, columns),
        out_shape=(
            jax.ShapeDtypeStruct((8, TILE, TILE), jnp.float32),
            jax.ShapeDtypeStruct((TILE, TILE), jnp.float32),
        ),
        in_specs=[pl.BlockSpec(memory_space=pltpu.SMEM), vmem, vmem, vmem],
        out_specs=(vmem, vmem),
        scratch_shapes=[
            f32(10, ROWS, 128),
            f32(10, ROWS, 128),
            f32(ROWS, 128),
            f32(ROWS, 128),
            f32(SUB, 32, 128),
            f32(SUB, 32, 128),
            pltpu.VMEM((8, 128), jnp.int32),
            pltpu.VMEM((3, SUB, 8, 128), jnp.int32),
            pltpu.VMEM((5, 8, 128), jnp.int32),
        ]
        + [f32(SUB, 16, 128)] * 6
        + [f32(ROWS, 128)] * 2
        + [pltpu.SemaphoreType.DMA((7,)), pltpu.SemaphoreType.DMA((7,))],
        compiler_params=pltpu.CompilerParams(
            collective_id=0, has_side_effects=True, vmem_limit_bytes=32 * 1024 * 1024
        ),
    )(neighbours, state.reshape(8, TILE, TILE), surface.reshape(TILE, TILE), wet)
    return new_state.reshape(1, 4, 2, TILE * TILE), new_surface.reshape(1, TILE * TILE)


def solution(mesh):
    spec = P(("tiles", "sub"))
    return jax.shard_map(
        functools.partial(shards, mesh.shape["tiles"]),
        mesh=mesh,
        in_specs=(spec, spec, spec, spec),
        out_specs=(spec, spec),
        check_vma=False,
    )
```

```python
import functools

import jax
import jax.numpy as jnp
from jax import lax
from jax.experimental import pallas as pl
from jax.experimental.pallas import tpu as pltpu
from jax.sharding import PartitionSpec as P

MESH = pl.DeviceIdType.MESH
TILE = 60
STEPS = 2
SUBCYCLES = 4
SUB = 8

time_step = 0.2
mixing = 0.02
coriolis = 0.5
gravity_step = 0.25
depth_step = 0.25

TOP = 24
ROWS = 112
ETA, WET = 8, 9
ITEMS = (
    [(4 + i, 17 * i, 17) for i in range(4)]
    + [(ETA, 68, 16), (WET, 84, 16)]
    + [(i, 100 + 4 * i, 4) for i in range(4)]
)
QUARTERS = (0, 16, 28, 44)


def lanes(shape):
    return lax.broadcasted_iota(jnp.int32, shape, len(shape) - 1)


def turn(x, shift):
    shift %= 128
    return pltpu.roll(x, shift, x.ndim - 1) if shift else x


def within(lane, first, count):
    return (lane >= first) & (lane < first + count)


def pack(D, ns, sides):
    def both(item, north, south, count):
        return D[item, TOP + north : TOP + north + count] + turn(D[item, TOP + south : TOP + south + count], 64)

    for i in range(4):
        ns[i, 0:16] = both(4 + i, 0, 43, 16)
        ns[6, 4 * i : 4 * i + 4] = both(i, 0, 56, 4)
        ns[7, i : i + 1] = both(4 + i, 16, 59, 1)
    ns[4, 0:16] = both(ETA, 0, 44, 16)
    ns[5, 0:16] = both(WET, 0, 44, 16)
    ns[7, 4:16] = jnp.zeros((12, 128), jnp.float32)
    lane = lanes((TILE, 128))
    east = west = jnp.zeros((TILE, 128), jnp.float32)
    for item, first, depth in ITEMS:
        whole = D[item, TOP : TOP + TILE]
        here = within(lane, first, depth)
        east = jnp.where(here, turn(whole, first - (TILE - depth)), east)
        west = jnp.where(here, turn(whole, first), west)
    for q, row in enumerate(QUARTERS):
        sides[0, q, 0:16] = east[row : row + 16]
        sides[1, q, 0:16] = west[row : row + 16]


def take(table, index):
    out = jnp.full((SUB, 128), -1.0, jnp.float32)
    for k in range(SUB):
        out = jnp.where(index == k, jnp.broadcast_to(table[k : k + 1], (SUB, 128)), out)
    return out


def wanted(own_in, side_in, me, lists):
    def column(held, direction):
        return jnp.concatenate([held[r, 16 + direction : 17 + direction] for r in range(SUB)], 0)

    north, east, south, west = (column(own_in, direction) for direction in range(4))
    beside = jnp.where(lax.rem(me, 2) == 0, east, west)
    up = jnp.where(north >= 0, take(beside, north), take(column(side_in, 0), beside))
    down = jnp.where(south >= 0, take(beside, south), take(column(side_in, 2), beside))
    lists[0] = jnp.where(lanes((SUB, 128)) < 64, south, north)
    lists[1] = beside
    lists[2] = jnp.where(me >= 4, up, down)


def unpack(D, got, eb, wb):
    for held, odd in ((eb, 0), (wb, 1)):
        held[8:24] = got[6 + odd, 32:48]
        for q, row in enumerate(QUARTERS):
            held[TOP + row : TOP + row + 16] = got[2 * q + odd, 16:32]
        held[84:100] = got[odd, 32:48]

    def put(item, rows, north, south):
        count = rows.shape[0]
        tile = lanes((count, 128)) < TILE
        D[item, TOP + north : TOP + north + count] = jnp.where(tile, turn(rows, 64), 0.0)
        D[item, TOP + south : TOP + south + count] = jnp.where(tile, rows, 0.0)

    for i in range(4):
        put(4 + i, got[i, 0:16], -17, 60)
        put(4 + i, got[7, i : i + 1], -1, 76)
        put(i, got[6, 4 * i : 4 * i + 4], -4, 60)
    put(ETA, got[4, 0:16], -16, 60)
    put(WET, got[5, 0:16], -16, 60)

    for item, first, depth in ITEMS:
        beyond = min(depth, 16)
        begin, count = TOP - beyond, TILE + 2 * beyond
        lane = lanes((count, 128))
        east = turn(eb[begin : begin + count], TILE - first)
        west = turn(wb[begin : begin + count], 128 - depth - first)
        sides = jnp.where(within(lane, TILE, depth), east, jnp.where(lane >= 128 - depth, west, 0.0))
        D[item, begin : begin + count] = D[item, begin : begin + count] + sides


def clinic(D, N, item, begin, count):
    level = item % 2

    def at(which, shift=0):
        return D[which, begin + shift : begin + shift + count]

    mid, north, south = at(item), at(item, -1), at(item, 1)
    wet = at(WET)
    u, v = at(4 + level), at(6 + level)
    right, left = turn(mid, -1), turn(mid, 1)
    cross = 2.0 * (north + south) - 8.0 * mid
    smooth = (
        20.0 * mid
        - 8.0 * (north + south)
        + at(item, -2)
        + at(item, 2)
        + turn(cross + right, -1)
        + turn(cross + left, 1)
    )
    tend = -(u * ((right - left) * 0.5) + v * ((south - north) * 0.5)) - mixing * smooth
    if item // 2 == 2:
        tend = tend + coriolis * v
    if item // 2 == 3:
        tend = tend - coriolis * u
    N[item, begin : begin + count] = (mid + time_step * tend) * wet
    lane = lanes((2, 128))
    for row in (TOP - 1, TOP + TILE - 1):
        swapped = jnp.concatenate([D[item, row + 1 : row + 2], D[item, row : row + 1]], 0)
        diagonal = jnp.where(
            (lane == 0) | (lane == TILE),
            turn(swapped, 1),
            jnp.where((lane == 127) | (lane == TILE - 1), turn(swapped, -1), 0.0),
        )
        N[item, row : row + 2] += (2.0 * time_step * mixing) * diagonal * D[WET, row : row + 2]


def tropic(heights, norths, wet_at, eta, zonal, meridional, begin, count):
    for _ in range(SUBCYCLES):
        heights[begin : begin + count] = eta
        norths[begin : begin + count] = meridional

        def a(shift):
            return heights[begin + shift : begin + shift + count]

        def c(shift):
            return norths[begin + shift : begin + shift + count]

        new_u = zonal - (gravity_step * 0.5) * (turn(eta, -1) - turn(eta, 1))
        new_v = meridional - (gravity_step * 0.5) * (a(1) - a(-1))
        along = (c(1) - c(-1)) - (gravity_step * 0.5) * ((a(2) - eta) - (eta - a(-2)))
        spread = (turn(new_u, -1) - turn(new_u, 1)) + along
        wet = wet_at(begin, count)
        eta = (eta - (depth_step * 0.5) * spread) * wet
        zonal, meridional = new_u * wet, new_v * wet
    return eta, zonal, meridional


def kernel(
    columns,
    near,
    state,
    surface,
    wet,
    new_state,
    new_surface,
    D,
    N,
    heights,
    norths,
    ns,
    sides,
    own_in,
    side_in,
    lists,
    out,
    got,
    eb,
    wb,
    sent,
    came,
):
    column, me = lax.axis_index("tiles"), lax.axis_index("sub")
    half, odd = me // 2, lax.rem(me, 2)
    after, before = lax.rem(column + 1, columns), lax.rem(column + columns - 1, columns)
    source = lax.rem(column + columns + 1 - 2 * odd, columns)
    others = [lax.rem(me + k, SUB) for k in (4, 3, 5, 2, 6, 1, 7)]
    quarters = [lax.rem(half + k, 4) for k in (2, 1, 3, 0)]

    barrier = pltpu.get_barrier_semaphore()
    for r in others:
        pl.semaphore_signal(barrier, inc=1, device_id=(column, r), device_id_type=MESH)
    for k in range(SUB):
        pl.semaphore_signal(barrier, inc=1, device_id=(source, lax.rem(me + k, SUB)), device_id_type=MESH)

    row = lax.broadcasted_iota(jnp.int32, (8, 128), 0)
    mine = jnp.full((8, 128), -1, jnp.int32)
    for direction, base in enumerate((column, column + 1, column, column - 1)):
        listed = near[0, direction]
        slot = jnp.where(listed >= 0, listed - base * SUB, -1)
        mine = jnp.where(row == direction, slot, mine)
    mine = mine.astype(jnp.float32)
    for m in range(SUB):
        ns[m, 16:24] = mine
    for q in range(4):
        sides[0, q, 16:24] = mine
        sides[1, q, 16:24] = mine

    D[...] = jnp.zeros_like(D)
    ocean = wet[...]
    D[WET, TOP : TOP + TILE, 0:TILE] = ocean
    D[ETA, TOP : TOP + TILE, 0:TILE] = surface[...] * ocean
    for item in range(8):
        D[item, TOP : TOP + TILE, 0:TILE] = state[item] * ocean
    pack(D, ns, sides)
    own_in[me] = ns[me]

    def send(source_ref, target, kind, device):
        pltpu.make_async_remote_copy(
            src_ref=source_ref,
            dst_ref=target,
            send_sem=sent.at[kind],
            recv_sem=came.at[kind],
            device_id=device,
            device_id_type=MESH,
        ).start()

    def wait(ref, semaphore):
        pltpu.make_async_copy(ref, ref, semaphore).wait()

    pl.semaphore_wait(barrier, 15)
    for q in quarters:
        send(sides.at[0, q], side_in.at[me], 1, (after, 2 * q + 1))
        send(sides.at[1, q], side_in.at[me], 1, (before, 2 * q))
    for r in others:
        send(ns.at[r], own_in.at[me], 0, (column, r))

    seven, eight = pl.ds(0, SUB - 1), pl.ds(0, SUB)
    wait(own_in.at[seven], came.at[0])
    wait(side_in.at[eight], came.at[1])
    wanted(own_in, side_in, me, lists)

    def picked(which, r, held):
        want = jnp.broadcast_to(lists[which, pl.ds(r, 1)], (8, 128))
        parts = [jnp.zeros((8, 128), jnp.float32)] * 2
        for k in range(SUB):
            hit = want == k
            parts = [jnp.where(hit, held[k, 8 * i : 8 * i + 8], parts[i]) for i in range(2)]
        return parts

    def fill(target, r):
        for which, held in enumerate((own_in, side_in, side_in)):
            for i, part in enumerate(picked(which, r, held)):
                target[r, 16 * which + 8 * i : 16 * which + 8 * i + 8] = part

    for r in others:
        fill(out, r)
        send(out.at[r], got.at[me], 2, (column, r))
    fill(got, me)
    wait(got.at[seven], came.at[2])

    unpack(D, got, eb, wb)
    N[...] = jnp.zeros_like(N)
    heights[...] = jnp.zeros_like(heights)
    norths[...] = jnp.zeros_like(norths)
    weights = (2.0 / 6.0, 4.0 / 6.0)
    fields, other = D, N
    wet_at = lambda begin, count: D[WET, begin : begin + count]
    for step in range(STEPS):
        begin, count = ((8, 96), (16, 80))[step]
        tracer = ((16, 72), (24, 64))[step]
        for item in range(4):
            clinic(fields, other, item, *tracer)
        for item in range(4, 8):
            clinic(fields, other, item, begin, count)
        rows = slice(begin, begin + count)
        old_u = weights[0] * other[4, rows] + weights[1] * other[5, rows]
        old_v = weights[0] * other[6, rows] + weights[1] * other[7, rows]
        eta, zonal, meridional = tropic(heights, norths, wet_at, fields[ETA, rows], old_u, old_v, begin, count)
        other[ETA, rows] = eta
        other[WET] = fields[WET]
        for level in range(2):
            other[4 + level, rows] += zonal - old_u
            other[6 + level, rows] += meridional - old_v
        fields, other = other, fields

    for item in range(8):
        new_state[item] = fields[item, TOP : TOP + TILE, 0:TILE]
    new_surface[...] = fields[ETA, TOP : TOP + TILE, 0:TILE]

    wait(own_in.at[seven], sent.at[0])
    wait(side_in.at[eight], sent.at[1])
    wait(got.at[seven], sent.at[2])


def shards(columns, state, surface, land_mask, neighbours):
    wet = land_mask.reshape(TILE, TILE).astype(jnp.float32)
    vmem = pl.BlockSpec(memory_space=pltpu.VMEM)
    f32 = lambda *shape: pltpu.VMEM(shape, jnp.float32)
    new_state, new_surface = pl.pallas_call(
        functools.partial(kernel, columns),
        out_shape=(
            jax.ShapeDtypeStruct((8, TILE, TILE), jnp.float32),
            jax.ShapeDtypeStruct((TILE, TILE), jnp.float32),
        ),
        in_specs=[pl.BlockSpec(memory_space=pltpu.SMEM), vmem, vmem, vmem],
        out_specs=(vmem, vmem),
        scratch_shapes=[
            f32(10, ROWS, 128),
            f32(10, ROWS, 128),
            f32(ROWS, 128),
            f32(ROWS, 128),
            f32(SUB, 24, 128),
            f32(2, 4, 24, 128),
            f32(SUB, 24, 128),
            f32(SUB, 24, 128),
            f32(3, 8, 128),
            f32(SUB, 48, 128),
            f32(SUB, 48, 128),
            f32(ROWS, 128),
            f32(ROWS, 128),
            pltpu.SemaphoreType.DMA((3,)),
            pltpu.SemaphoreType.DMA((3,)),
        ],
        compiler_params=pltpu.CompilerParams(
            collective_id=0, has_side_effects=True, vmem_limit_bytes=32 * 1024 * 1024
        ),
    )(neighbours, state.reshape(8, TILE, TILE), surface.reshape(TILE, TILE), wet)
    return new_state.reshape(1, 4, 2, TILE * TILE), new_surface.reshape(1, TILE * TILE)


def solution(mesh):
    spec = P(("tiles", "sub"))
    return jax.shard_map(
        functools.partial(shards, mesh.shape["tiles"]),
        mesh=mesh,
        in_specs=(spec, spec, spec, spec),
        out_specs=(spec, spec),
        check_vma=False,
    )
```

```python
import functools

import jax
import jax.numpy as jnp
from jax import lax
from jax.experimental import pallas as pl
from jax.experimental.pallas import tpu as pltpu
from jax.sharding import PartitionSpec as P

MESH = pl.DeviceIdType.MESH
TILE = 60
STEPS = 2
SUBCYCLES = 4
SUB = 8

time_step = 0.2
mixing = 0.02
coriolis = 0.5
gravity_step = 0.25
depth_step = 0.25

TOP = 24
ROWS = 112
ETA, WET = 8, 9
ITEMS = (
    [(4 + i, 17 * i, 17) for i in range(4)]
    + [(ETA, 68, 16), (WET, 84, 16)]
    + [(i, 100 + 4 * i, 4) for i in range(4)]
)
QUARTERS = (0, 16, 28, 44)
LISTED = 116


def lanes(shape):
    return lax.broadcasted_iota(jnp.int32, shape, len(shape) - 1)


def turn(x, shift):
    shift %= 128
    return pltpu.roll(x, shift, x.ndim - 1) if shift else x


def within(lane, first, count):
    return (lane >= first) & (lane < first + count)


def spread(tile_of, last, write):
    lane = lanes((8, 128))
    for b in range(8):
        row = 8 * b + lax.broadcasted_iota(jnp.int32, (8, 128), 0)
        begin = TILE * row
        tile = (begin + ((lane - begin) & 127)) >> 7
        first = (480 * b) // 128
        flat = jnp.zeros((8, 128), jnp.float32)
        for a in range(first, min((480 * b + 479) // 128, 28) + 1):
            flat = jnp.where(tile == a, jnp.broadcast_to(last if a == 28 else tile_of(a), (8, 128)), flat)
        flat = jnp.where(row & 1 == 1, turn(flat, 64), flat)
        rows = pltpu.roll(flat, (-480 * b) % 128, 1, stride=4, stride_axis=0)
        count = min(8, TILE - 8 * b)
        write(8 * b, count, jnp.where(lane < TILE, rows, 0.0)[0:count])


def flatten(rows, b):
    row = lax.broadcasted_iota(jnp.int32, (8, 128), 0)
    rows = jnp.where(row & 1 == 1, turn(rows, 480 * b + 60), turn(rows, 480 * b))
    rows = jnp.where(row & 2 == 2, turn(rows, 120), rows)
    return jnp.where(row & 4 == 4, turn(rows, 240), rows)


def joined(row_of, a, height):
    lane = lanes((height, 128)) + 128 * a
    first = (128 * a) // TILE
    out = row_of(first)
    for i in range(first + 1, min((128 * a + 127) // TILE, TILE - 1) + 1):
        out = jnp.where(lane < TILE * i, out, row_of(i))
    return out


def pack(D, ns, sides):
    def both(item, north, south, count):
        return D[item, TOP + north : TOP + north + count] + turn(D[item, TOP + south : TOP + south + count], 64)

    for i in range(4):
        ns[i, 0:16] = both(4 + i, 0, 43, 16)
        ns[6, 4 * i : 4 * i + 4] = both(i, 0, 56, 4)
        ns[7, i : i + 1] = both(4 + i, 16, 59, 1)
    ns[4, 0:16] = both(ETA, 0, 44, 16)
    ns[5, 0:16] = both(WET, 0, 44, 16)
    ns[7, 4:16] = jnp.zeros((12, 128), jnp.float32)
    lane = lanes((TILE, 128))
    east = west = jnp.zeros((TILE, 128), jnp.float32)
    for item, first, depth in ITEMS:
        whole = D[item, TOP : TOP + TILE]
        here = within(lane, first, depth)
        east = jnp.where(here, turn(whole, first - (TILE - depth)), east)
        west = jnp.where(here, turn(whole, first), west)
    for q, row in enumerate(QUARTERS):
        sides[0, q, 0:16] = east[row : row + 16]
        sides[1, q, 0:16] = west[row : row + 16]


def take(table, index):
    out = jnp.full((SUB, 128), -1.0, jnp.float32)
    for k in range(SUB):
        out = jnp.where(index == k, jnp.broadcast_to(table[k : k + 1], (SUB, 128)), out)
    return out


def wanted(own_in, side_in, me, lists):
    def table(held):
        return jnp.concatenate([held[r, 0:1] for r in range(SUB)], 0)

    def column(rows, lane):
        return jnp.broadcast_to(rows[:, lane : lane + 1], (SUB, 128))

    own, side = table(own_in), table(side_in)
    north, east, south, west = (column(own, TILE + direction) for direction in range(4))
    beside = jnp.where(lax.rem(me, 2) == 0, east, west)
    up = jnp.where(north >= 0, take(beside, north), take(column(side, LISTED), beside))
    down = jnp.where(south >= 0, take(beside, south), take(column(side, LISTED + 2), beside))
    lists[0] = jnp.where(lanes((SUB, 128)) < 64, south, north)
    lists[1] = beside
    lists[2] = jnp.where(me >= 4, up, down)


def unpack(D, got, eb, wb):
    for held, odd in ((eb, 0), (wb, 1)):
        held[8:24] = got[6 + odd, 32:48]
        for q, row in enumerate(QUARTERS):
            held[TOP + row : TOP + row + 16] = got[2 * q + odd, 16:32]
        held[84:100] = got[odd, 32:48]

    def put(item, rows, north, south):
        count = rows.shape[0]
        tile = lanes((count, 128)) < TILE
        D[item, TOP + north : TOP + north + count] = jnp.where(tile, turn(rows, 64), 0.0)
        D[item, TOP + south : TOP + south + count] = jnp.where(tile, rows, 0.0)

    for i in range(4):
        put(4 + i, got[i, 0:16], -17, 60)
        put(4 + i, got[7, i : i + 1], -1, 76)
        put(i, got[6, 4 * i : 4 * i + 4], -4, 60)
    put(ETA, got[4, 0:16], -16, 60)
    put(WET, got[5, 0:16], -16, 60)

    for item, first, depth in ITEMS:
        beyond = min(depth, 16)
        begin, count = TOP - beyond, TILE + 2 * beyond
        lane = lanes((count, 128))
        east = turn(eb[begin : begin + count], TILE - first)
        west = turn(wb[begin : begin + count], 128 - depth - first)
        sides = jnp.where(within(lane, TILE, depth), east, jnp.where(lane >= 128 - depth, west, 0.0))
        D[item, begin : begin + count] = D[item, begin : begin + count] + sides


def clinic(D, N, item, begin, count):
    level = item % 2

    def at(which, shift=0):
        return D[which, begin + shift : begin + shift + count]

    mid, north, south = at(item), at(item, -1), at(item, 1)
    wet = at(WET)
    u, v = at(4 + level), at(6 + level)
    right, left = turn(mid, -1), turn(mid, 1)
    cross = 2.0 * (north + south) - 8.0 * mid
    smooth = (
        20.0 * mid
        - 8.0 * (north + south)
        + at(item, -2)
        + at(item, 2)
        + turn(cross + right, -1)
        + turn(cross + left, 1)
    )
    tend = -(u * ((right - left) * 0.5) + v * ((south - north) * 0.5)) - mixing * smooth
    if item // 2 == 2:
        tend = tend + coriolis * v
    if item // 2 == 3:
        tend = tend - coriolis * u
    N[item, begin : begin + count] = (mid + time_step * tend) * wet
    lane = lanes((2, 128))
    for row in (TOP - 1, TOP + TILE - 1):
        swapped = jnp.concatenate([D[item, row + 1 : row + 2], D[item, row : row + 1]], 0)
        diagonal = jnp.where(
            (lane == 0) | (lane == TILE),
            turn(swapped, 1),
            jnp.where((lane == 127) | (lane == TILE - 1), turn(swapped, -1), 0.0),
        )
        N[item, row : row + 2] += (2.0 * time_step * mixing) * diagonal * D[WET, row : row + 2]


def tropic(heights, norths, wet_at, eta, zonal, meridional, begin, count):
    for _ in range(SUBCYCLES):
        heights[begin : begin + count] = eta
        norths[begin : begin + count] = meridional

        def a(shift):
            return heights[begin + shift : begin + shift + count]

        def c(shift):
            return norths[begin + shift : begin + shift + count]

        new_u = zonal - (gravity_step * 0.5) * (turn(eta, -1) - turn(eta, 1))
        new_v = meridional - (gravity_step * 0.5) * (a(1) - a(-1))
        along = (c(1) - c(-1)) - (gravity_step * 0.5) * ((a(2) - eta) - (eta - a(-2)))
        spread = (turn(new_u, -1) - turn(new_u, 1)) + along
        wet = wet_at(begin, count)
        eta = (eta - (depth_step * 0.5) * spread) * wet
        zonal, meridional = new_u * wet, new_v * wet
    return eta, zonal, meridional


def kernel(
    columns,
    near_in,
    state_in,
    surface_in,
    mask_in,
    new_state,
    new_surface,
    state,
    surface,
    mask,
    tails,
    turned,
    near,
    loaded,
    D,
    N,
    heights,
    norths,
    ns,
    sides,
    own_in,
    side_in,
    lists,
    out,
    got,
    eb,
    wb,
    sent,
    came,
):
    column, me = lax.axis_index("tiles"), lax.axis_index("sub")
    half, odd = me // 2, lax.rem(me, 2)
    after, before = lax.rem(column + 1, columns), lax.rem(column + columns - 1, columns)
    source = lax.rem(column + columns + 1 - 2 * odd, columns)
    others = [lax.rem(me + k, SUB) for k in (4, 3, 5, 2, 6, 1, 7)]
    quarters = [lax.rem(half + k, 4) for k in (2, 1, 3, 0)]

    barrier = pltpu.get_barrier_semaphore()
    for k in (4, 3, 5, 2, 6, 1, 7, 0):
        r = lax.rem(me + k, SUB)
        pl.semaphore_signal(barrier, inc=1, device_id=(source, r), device_id_type=MESH)
        if k:
            pl.semaphore_signal(barrier, inc=1, device_id=(column, r), device_id_type=MESH)

    loads = [
        pltpu.make_async_copy(held, target, loaded.at[i])
        for i, (held, target) in enumerate(((mask_in, mask), (surface_in, surface), (state_in, state), (near_in, near)))
    ]
    for load in loads:
        load.start()
    D[...] = jnp.zeros_like(D)

    def put(item):
        def write(at, count, rows):
            if item != WET:
                rows = rows * D[WET, TOP + at : TOP + at + count]
            D[item, TOP + at : TOP + at + count] = rows

        return write

    loads[0].wait()
    tails[0:1, 0:16] = mask[0:1, 3584:3600].astype(jnp.float32)
    spread(lambda a: mask[0:1, 128 * a : 128 * a + 128].astype(jnp.float32), tails[0:1], put(WET))
    loads[1].wait()
    tails[1:2, 0:16] = surface[0:1, 3584:3600]
    spread(lambda a: surface[0:1, 128 * a : 128 * a + 128], tails[1:2], put(ETA))
    loads[2].wait()
    for field in range(4):
        tails[8 + 2 * field : 10 + 2 * field, 0:16] = state[0, field, :, 3584:3600]
        for level in range(2):
            item = 2 * field + level
            spread(
                lambda a, field=field, level=level: state[0, field, level : level + 1, 128 * a : 128 * a + 128],
                tails[8 + item : 9 + item],
                put(item),
            )
    pack(D, ns, sides)
    loads[3].wait()
    lane = lanes((1, 128))
    mine = jnp.zeros((1, 128), jnp.float32)
    for direction, base in enumerate((column, column + 1, column, column - 1)):
        listed = near[0, direction]
        slot = jnp.where(listed >= 0, listed - base * SUB, -1).astype(jnp.float32)
        mine = jnp.where(lane == TILE + direction, slot, mine)
    for m in range(SUB):
        ns[m, 0:1] += mine
    mine = turn(mine, LISTED - TILE)
    for q in range(4):
        sides[0, q, 0:1] += mine
        sides[1, q, 0:1] += mine
    own_in[me] = ns[me]

    def send(source_ref, target, kind, device):
        pltpu.make_async_remote_copy(
            src_ref=source_ref,
            dst_ref=target,
            send_sem=sent.at[kind],
            recv_sem=came.at[kind],
            device_id=device,
            device_id_type=MESH,
        ).start()

    def wait(ref, semaphore):
        pltpu.make_async_copy(ref, ref, semaphore).wait()

    pl.semaphore_wait(barrier, 15)
    for q in quarters:
        send(sides.at[0, q], side_in.at[me], 1, (after, 2 * q + 1))
        send(sides.at[1, q], side_in.at[me], 1, (before, 2 * q))
    for r in others:
        send(ns.at[r], own_in.at[me], 0, (column, r))

    seven, eight = pl.ds(0, SUB - 1), pl.ds(0, SUB)
    wait(own_in.at[seven], came.at[0])
    wait(side_in.at[eight], came.at[1])
    wanted(own_in, side_in, me, lists)

    def picked(which, r, held):
        want = jnp.broadcast_to(lists[which, pl.ds(r, 1)], (8, 128))
        parts = [jnp.zeros((8, 128), jnp.float32)] * 2
        for k in range(SUB):
            hit = want == k
            parts = [jnp.where(hit, held[k, 8 * i : 8 * i + 8], parts[i]) for i in range(2)]
        return parts

    outer = (half == 0) | (half == 3)
    first = lambda count, rows: got.at[pl.ds(0, count), pl.ds(0, rows)]

    def fill(target, r, pieces):
        for which, held in enumerate((own_in, side_in, side_in)[:pieces]):
            for i, part in enumerate(picked(which, r, held)):
                target[r, 16 * which + 8 * i : 16 * which + 8 * i + 8] = part

    def second_hop(kind, pieces):
        rows = pl.ds(0, 16 * pieces)
        for r in others:
            fill(out, r, pieces)
            send(out.at[r, rows], got.at[me, rows], kind, (column, r))
        fill(got, me, pieces)
        wait(first(4 - (kind == 2), 48), came.at[2])
        wait(first(4 - (kind == 3), 32), came.at[3])

    pl.when(outer)(lambda: second_hop(2, 3))
    pl.when(jnp.logical_not(outer))(lambda: second_hop(3, 2))

    unpack(D, got, eb, wb)
    N[...] = jnp.zeros_like(N)
    heights[...] = jnp.zeros_like(heights)
    norths[...] = jnp.zeros_like(norths)
    weights = (2.0 / 6.0, 4.0 / 6.0)
    fields, other = D, N
    wet_at = lambda begin, count: D[WET, begin : begin + count]
    for step in range(STEPS):
        begin, count = ((8, 96), (16, 80))[step]
        tracer = ((16, 72), (24, 64))[step]
        for item in range(4):
            clinic(fields, other, item, *tracer)
        for item in range(4, 8):
            clinic(fields, other, item, begin, count)
        rows = slice(begin, begin + count)
        old_u = weights[0] * other[4, rows] + weights[1] * other[5, rows]
        old_v = weights[0] * other[6, rows] + weights[1] * other[7, rows]
        eta, zonal, meridional = tropic(heights, norths, wet_at, fields[ETA, rows], old_u, old_v, begin, count)
        other[ETA, rows] = eta
        other[WET] = fields[WET]
        for level in range(2):
            other[4 + level, rows] += zonal - old_u
            other[6 + level, rows] += meridional - old_v
        fields, other = other, fields

    for item in range(8):
        new_state[item] = fields[item, TOP : TOP + TILE, 0:TILE]
    for b in range(8):
        turned[8 * b : 8 * b + 8] = flatten(fields[ETA, TOP + 8 * b : TOP + 8 * b + 8], b)
    for a in range(29):
        width = min(128, TILE * TILE - 128 * a)
        tile = joined(lambda i: turned[i : i + 1], a, 1)
        new_surface[0:1, 128 * a : 128 * a + width] = tile[:, 0:width]

    wait(own_in.at[seven], sent.at[0])
    wait(side_in.at[eight], sent.at[1])
    pl.when(outer)(lambda: wait(first(7, 48), sent.at[2]))
    pl.when(jnp.logical_not(outer))(lambda: wait(first(7, 32), sent.at[3]))


def shards(columns, state, surface, land_mask, neighbours):
    hbm, vmem = pl.BlockSpec(memory_space=pltpu.HBM), pl.BlockSpec(memory_space=pltpu.VMEM)
    f32 = lambda *shape: pltpu.VMEM(shape, jnp.float32)
    new_state, new_surface = pl.pallas_call(
        functools.partial(kernel, columns),
        out_shape=(
            jax.ShapeDtypeStruct((8, TILE, TILE), jnp.float32),
            jax.ShapeDtypeStruct(surface.shape, jnp.float32),
        ),
        in_specs=[hbm] * 4,
        out_specs=(vmem, vmem),
        scratch_shapes=[
            f32(*state.shape),
            f32(*surface.shape),
            pltpu.VMEM(surface.shape, jnp.int32),
            f32(16, 128),
            f32(64, 128),
            pltpu.SMEM((1, 4), jnp.int32),
            pltpu.SemaphoreType.DMA((4,)),
            f32(10, ROWS, 128),
            f32(10, ROWS, 128),
            f32(ROWS, 128),
            f32(ROWS, 128),
            f32(SUB, 16, 128),
            f32(2, 4, 16, 128),
            f32(SUB, 16, 128),
            f32(SUB, 16, 128),
            f32(3, 8, 128),
            f32(SUB, 48, 128),
            f32(SUB, 48, 128),
            f32(ROWS, 128),
            f32(ROWS, 128),
            pltpu.SemaphoreType.DMA((4,)),
            pltpu.SemaphoreType.DMA((4,)),
        ],
        compiler_params=pltpu.CompilerParams(
            collective_id=0, has_side_effects=True, vmem_limit_bytes=56 * 1024 * 1024
        ),
    )(neighbours, state, surface, land_mask)
    return new_state.reshape(state.shape), new_surface


def solution(mesh):
    spec = P(("tiles", "sub"))
    return jax.shard_map(
        functools.partial(shards, mesh.shape["tiles"]),
        mesh=mesh,
        in_specs=(spec, spec, spec, spec),
        out_specs=(spec, spec),
        check_vma=False,
    )
```

```python
import functools

import jax
import jax.numpy as jnp
from jax import lax
from jax.experimental import pallas as pl
from jax.experimental.pallas import tpu as pltpu
from jax.sharding import PartitionSpec as P

MESH = pl.DeviceIdType.MESH
TILE = 60
STEPS = 2
SUBCYCLES = 4
SUB = 8

time_step = 0.2
mixing = 0.02
coriolis = 0.5
gravity_step = 0.25
depth_step = 0.25

TOP = 24
ROWS = 112
ETA, WET = 8, 9
ITEMS = (
    [(4 + i, 17 * i, 17) for i in range(4)]
    + [(ETA, 68, 16), (WET, 84, 16)]
    + [(i, 100 + 4 * i, 4) for i in range(4)]
)
HALVES = (0, 28)
LISTED = 116


def lanes(shape):
    return lax.broadcasted_iota(jnp.int32, shape, len(shape) - 1)


def turn(x, shift):
    shift %= 128
    return pltpu.roll(x, shift, x.ndim - 1) if shift else x


def within(lane, first, count):
    return (lane >= first) & (lane < first + count)


def spread(tile_of, last, write):
    lane = lanes((8, 128))
    for b in range(8):
        row = 8 * b + lax.broadcasted_iota(jnp.int32, (8, 128), 0)
        begin = TILE * row
        tile = (begin + ((lane - begin) & 127)) >> 7
        first = (480 * b) // 128
        flat = jnp.zeros((8, 128), jnp.float32)
        for a in range(first, min((480 * b + 479) // 128, 28) + 1):
            flat = jnp.where(tile == a, jnp.broadcast_to(last if a == 28 else tile_of(a), (8, 128)), flat)
        flat = jnp.where(row & 1 == 1, turn(flat, 64), flat)
        rows = pltpu.roll(flat, (-480 * b) % 128, 1, stride=4, stride_axis=0)
        count = min(8, TILE - 8 * b)
        write(8 * b, count, jnp.where(lane < TILE, rows, 0.0)[0:count])


def flatten(rows, b):
    row = lax.broadcasted_iota(jnp.int32, (8, 128), 0)
    rows = jnp.where(row & 1 == 1, turn(rows, 480 * b + 60), turn(rows, 480 * b))
    rows = jnp.where(row & 2 == 2, turn(rows, 120), rows)
    return jnp.where(row & 4 == 4, turn(rows, 240), rows)


def joined(row_of, a, height):
    lane = lanes((height, 128)) + 128 * a
    first = (128 * a) // TILE
    out = row_of(first)
    for i in range(first + 1, min((128 * a + 127) // TILE, TILE - 1) + 1):
        out = jnp.where(lane < TILE * i, out, row_of(i))
    return out


def pack(D, ns, sides):
    def both(item, north, south, count):
        return D[item, TOP + north : TOP + north + count] + turn(D[item, TOP + south : TOP + south + count], 64)

    for i in range(4):
        ns[i // 2, 16 * (i % 2) : 16 * (i % 2) + 16] = both(4 + i, 0, 43, 16)
        ns[3, 4 * i : 4 * i + 4] = both(i, 0, 56, 4)
        ns[3, 16 + i : 17 + i] = both(4 + i, 16, 59, 1)
    ns[2, 0:16] = both(ETA, 0, 44, 16)
    ns[2, 16:32] = both(WET, 0, 44, 16)
    ns[3, 20:32] = jnp.zeros((12, 128), jnp.float32)
    lane = lanes((TILE, 128))
    east = west = jnp.zeros((TILE, 128), jnp.float32)
    for item, first, depth in ITEMS:
        whole = D[item, TOP : TOP + TILE]
        here = within(lane, first, depth)
        east = jnp.where(here, turn(whole, first - (TILE - depth)), east)
        west = jnp.where(here, turn(whole, first), west)
    for half, row in enumerate(HALVES):
        sides[0, half] = east[row : row + 32]
        sides[1, half] = west[row : row + 32]


def take(table, index):
    out = jnp.full((SUB, 128), -1.0, jnp.float32)
    for k in range(SUB):
        out = jnp.where(index == k, jnp.broadcast_to(table[k : k + 1], (SUB, 128)), out)
    return out


def table(held):
    return jnp.concatenate([held[r, 0:1] for r in range(SUB)], 0)


def column_of(rows, lane):
    return jnp.broadcast_to(rows[:, lane : lane + 1], (SUB, 128))


def wanted(own_in, me, lists):
    own = table(own_in)
    north, east, south, west = (column_of(own, TILE + direction) for direction in range(4))
    beside = jnp.where(lax.rem(me, 2) == 0, east, west)
    lists[0] = jnp.where(lanes((SUB, 128)) < 64, south, north)
    lists[1] = beside
    beyond = jnp.where(lax.rem(me, 4) >= 2, north, south)
    lists[3] = beyond
    lists[4] = take(beside, beyond)


def corners(side_in, me, lists):
    side = table(side_in)
    around = jnp.where(lax.rem(me, 4) >= 2, column_of(side, LISTED), column_of(side, LISTED + 2))
    lists[2] = jnp.where(lists[3] >= 0, lists[4], take(around, lists[1]))


def unpack_ends(D, got):
    def put(item, rows, north, south):
        count = rows.shape[0]
        tile = lanes((count, 128)) < TILE
        D[item, TOP + north : TOP + north + count] = jnp.where(tile, turn(rows, 64), 0.0)
        D[item, TOP + south : TOP + south + count] = jnp.where(tile, rows, 0.0)

    for i in range(4):
        put(4 + i, got[i // 2, 16 * (i % 2) : 16 * (i % 2) + 16], -17, 60)
        put(4 + i, got[3, 16 + i : 17 + i], -1, 76)
        put(i, got[3, 4 * i : 4 * i + 4], -4, 60)
    put(ETA, got[2, 0:16], -16, 60)
    put(WET, got[2, 16:32], -16, 60)


def unpack_sides(D, got, eb, wb):
    for held, odd in ((eb, 0), (wb, 1)):
        held[8:24] = got[2 + odd, 64:80]
        for half, row in enumerate(HALVES):
            held[TOP + row : TOP + row + 32] = got[2 * half + odd, 32:64]
        held[84:100] = got[odd, 64:80]

    for item, first, depth in ITEMS:
        beyond = min(depth, 16)
        begin, count = TOP - beyond, TILE + 2 * beyond
        lane = lanes((count, 128))
        east = turn(eb[begin : begin + count], TILE - first)
        west = turn(wb[begin : begin + count], 128 - depth - first)
        sides = jnp.where(within(lane, TILE, depth), east, jnp.where(lane >= 128 - depth, west, 0.0))
        D[item, begin : begin + count] = D[item, begin : begin + count] + sides


def clinic(D, N, wets, item, begin, count):
    level = item % 2

    def at(which, shift=0):
        return D[which, begin + shift : begin + shift + count]

    mid, north, south = at(item), at(item, -1), at(item, 1)
    half_u = (0.5 * time_step) * at(4 + level)
    half_v = (0.5 * time_step) * at(6 + level)
    right, left = turn(mid, -1), turn(mid, 1)
    pair = north + south
    cross = 2.0 * pair - 8.0 * mid
    far = (at(item, -2) + at(item, 2)) + (turn(cross + right, -1) + turn(cross + left, 1))
    rate = time_step * mixing
    new = (1.0 - 20.0 * rate) * mid + (8.0 * rate) * pair - rate * far
    new = new - half_u * (right - left) - half_v * (south - north)
    if item // 2 == 2:
        new = new + (2.0 * coriolis) * half_v
    if item // 2 == 3:
        new = new - (2.0 * coriolis) * half_u
    N[item, begin : begin + count] = new * wets[begin : begin + count]
    lane = lanes((2, 128))
    for row in (TOP - 1, TOP + TILE - 1):
        swapped = jnp.concatenate([D[item, row + 1 : row + 2], D[item, row : row + 1]], 0)
        diagonal = jnp.where(
            (lane == 0) | (lane == TILE),
            turn(swapped, 1),
            jnp.where((lane == 127) | (lane == TILE - 1), turn(swapped, -1), 0.0),
        )
        N[item, row : row + 2] += (2.0 * rate) * diagonal * wets[row : row + 2]


def tropic(heights, norths, wet_at, eta, zonal, meridional, begin, count):
    for _ in range(SUBCYCLES):
        heights[begin : begin + count] = eta
        norths[begin : begin + count] = meridional

        def a(shift):
            return heights[begin + shift : begin + shift + count]

        def c(shift):
            return norths[begin + shift : begin + shift + count]

        new_u = zonal - (gravity_step * 0.5) * (turn(eta, -1) - turn(eta, 1))
        new_v = meridional - (gravity_step * 0.5) * (a(1) - a(-1))
        along = (c(1) - c(-1)) - (gravity_step * 0.5) * ((a(2) - eta) - (eta - a(-2)))
        spread = (turn(new_u, -1) - turn(new_u, 1)) + along
        wet = wet_at(begin, count)
        eta = (eta - (depth_step * 0.5) * spread) * wet
        zonal, meridional = new_u * wet, new_v * wet
    return eta, zonal, meridional


def kernel(
    columns,
    near_in,
    state_in,
    surface_in,
    mask_in,
    new_state,
    new_surface,
    state,
    surface,
    mask,
    tails,
    turned,
    near,
    loaded,
    D,
    N,
    heights,
    norths,
    ns,
    sides,
    own_in,
    side_in,
    lists,
    out,
    got,
    eb,
    wb,
    sent,
    came,
):
    column, me = lax.axis_index("tiles"), lax.axis_index("sub")
    quarter, odd = lax.rem(me, 4), lax.rem(me, 2)
    after, before = lax.rem(column + 1, columns), lax.rem(column + columns - 1, columns)
    source = lax.rem(column + columns + 1 - 2 * odd, columns)
    others = [lax.rem(me + k, SUB) for k in (4, 3, 5, 2, 6, 1, 7)]
    pairs = [lax.rem(me // 2 + k, 4) for k in (2, 1, 3, 0)]
    turns = 1 - 2 * lax.rem(column, 2)
    close = [lax.rem(me + SUB + turns * k, SUB) for k in (2, 1, -1)]

    barrier = pltpu.get_barrier_semaphore()
    for k in (4, 3, 5, 2, 6, 1, 7, 0):
        r = lax.rem(me + k, SUB)
        pl.semaphore_signal(barrier, inc=1, device_id=(source, r), device_id_type=MESH)
        if k:
            pl.semaphore_signal(barrier, inc=1, device_id=(column, r), device_id_type=MESH)

    loads = [
        pltpu.make_async_copy(held, target, loaded.at[i])
        for i, (held, target) in enumerate(((mask_in, mask), (surface_in, surface), (state_in, state), (near_in, near)))
    ]
    for load in loads:
        load.start()
    D[...] = jnp.zeros_like(D)

    def put(item):
        def write(at, count, rows):
            if item != WET:
                rows = rows * D[WET, TOP + at : TOP + at + count]
            D[item, TOP + at : TOP + at + count] = rows

        return write

    loads[0].wait()
    tails[0:1, 0:16] = mask[0:1, 3584:3600].astype(jnp.float32)
    spread(lambda a: mask[0:1, 128 * a : 128 * a + 128].astype(jnp.float32), tails[0:1], put(WET))
    loads[1].wait()
    tails[1:2, 0:16] = surface[0:1, 3584:3600]
    spread(lambda a: surface[0:1, 128 * a : 128 * a + 128], tails[1:2], put(ETA))
    loads[2].wait()
    for field in range(4):
        tails[8 + 2 * field : 10 + 2 * field, 0:16] = state[0, field, :, 3584:3600]
        for level in range(2):
            item = 2 * field + level
            spread(
                lambda a, field=field, level=level: state[0, field, level : level + 1, 128 * a : 128 * a + 128],
                tails[8 + item : 9 + item],
                put(item),
            )
    pack(D, ns, sides)
    loads[3].wait()
    lane = lanes((1, 128))
    mine = jnp.zeros((1, 128), jnp.float32)
    for direction, base in enumerate((column, column + 1, column, column - 1)):
        listed = near[0, direction]
        slot = jnp.where(listed >= 0, listed - base * SUB, -1).astype(jnp.float32)
        mine = jnp.where(lane == TILE + direction, slot, mine)
    for q in range(4):
        ns[q, 0:1] += mine
    mine = turn(mine, LISTED - TILE)
    for half in range(2):
        sides[0, half, 0:1] += mine
        sides[1, half, 0:1] += mine
    own_in[me] = ns[quarter]

    def send(source_ref, target, kind, device):
        pltpu.make_async_remote_copy(
            src_ref=source_ref,
            dst_ref=target,
            send_sem=sent.at[kind],
            recv_sem=came.at[kind],
            device_id=device,
            device_id_type=MESH,
        ).start()

    def wait(ref, semaphore):
        pltpu.make_async_copy(ref, ref, semaphore).wait()

    pl.semaphore_wait(barrier, 15)
    for pair in pairs:
        half = lax.rem(pair, 2)
        send(sides.at[0, half], side_in.at[me], 1, (after, 2 * pair + 1))
        send(sides.at[1, half], side_in.at[me], 1, (before, 2 * pair))
    for r in others:
        send(ns.at[lax.rem(r, 4)], own_in.at[me], 0, (column, r))

    N[...] = jnp.zeros_like(N)
    heights[...] = jnp.zeros_like(heights)
    norths[...] = jnp.zeros_like(norths)

    def fill(target, slot, r, which, held, begin, at, count):
        want = jnp.broadcast_to(lists[which, pl.ds(r, 1)], (8, 128))
        parts = [jnp.zeros((8, 128), jnp.float32)] * (count // 8)
        for k in range(SUB):
            hit = want == k
            for i in range(count // 8):
                parts[i] = jnp.where(hit, held[k, pl.ds(begin + 8 * i, 8)], parts[i])
        for i, part in enumerate(parts):
            target[slot, at + 8 * i : at + 8 * i + 8] = part

    def fill_sides(target, slot, r):
        fill(target, slot, r, 1, side_in, 0, 32, 32)
        fill(target, slot, r, 2, side_in, pl.multiple_of(16 * (quarter // 2), 16), 64, 16)

    seven, eight, three = pl.ds(0, SUB - 1), pl.ds(0, SUB), pl.ds(0, 3)
    ends, flanks = pl.ds(0, 32), pl.ds(32, 48)
    wait(own_in.at[seven], came.at[0])
    wanted(own_in, me, lists)
    for i, r in enumerate(close):
        fill(out, i, r, 0, own_in, 0, 0, 32)
        send(out.at[i, ends], got.at[quarter, ends], 2, (column, r))
    fill(got, quarter, me, 0, own_in, 0, 0, 32)

    wait(side_in.at[eight], came.at[1])
    corners(side_in, me, lists)
    for i, r in enumerate(close):
        fill_sides(out, i, r)
        send(out.at[i, flanks], got.at[quarter, flanks], 3, (column, r))
    fill_sides(got, quarter, me)

    wait(got.at[three, ends], came.at[2])
    unpack_ends(D, got)
    wait(got.at[three, flanks], came.at[3])
    unpack_sides(D, got, eb, wb)
    weights = (2.0 / 6.0, 4.0 / 6.0)
    fields, other = D, N
    wet_at = lambda begin, count: D[WET, begin : begin + count]
    for step in range(STEPS):
        begin, count = ((8, 96), (16, 80))[step]
        tracer = ((16, 72), (24, 64))[step]
        for item in range(4):
            clinic(fields, other, D.at[WET], item, *tracer)
        for item in range(4, 8):
            clinic(fields, other, D.at[WET], item, begin, count)
        rows = slice(begin, begin + count)
        old_u = weights[0] * other[4, rows] + weights[1] * other[5, rows]
        old_v = weights[0] * other[6, rows] + weights[1] * other[7, rows]
        eta, zonal, meridional = tropic(heights, norths, wet_at, fields[ETA, rows], old_u, old_v, begin, count)
        other[ETA, rows] = eta
        for level in range(2):
            other[4 + level, rows] += zonal - old_u
            other[6 + level, rows] += meridional - old_v
        fields, other = other, fields

    for item in range(8):
        new_state[item] = fields[item, TOP : TOP + TILE, 0:TILE]
    for b in range(8):
        turned[8 * b : 8 * b + 8] = flatten(fields[ETA, TOP + 8 * b : TOP + 8 * b + 8], b)
    for a in range(29):
        width = min(128, TILE * TILE - 128 * a)
        tile = joined(lambda i: turned[i : i + 1], a, 1)
        new_surface[0:1, 128 * a : 128 * a + width] = tile[:, 0:width]

    wait(own_in.at[seven], sent.at[0])
    wait(side_in.at[eight], sent.at[1])
    wait(got.at[three, ends], sent.at[2])
    wait(got.at[three, flanks], sent.at[3])


def shards(columns, state, surface, land_mask, neighbours):
    hbm, vmem = pl.BlockSpec(memory_space=pltpu.HBM), pl.BlockSpec(memory_space=pltpu.VMEM)
    f32 = lambda *shape: pltpu.VMEM(shape, jnp.float32)
    new_state, new_surface = pl.pallas_call(
        functools.partial(kernel, columns),
        out_shape=(
            jax.ShapeDtypeStruct((8, TILE, TILE), jnp.float32),
            jax.ShapeDtypeStruct(surface.shape, jnp.float32),
        ),
        in_specs=[hbm] * 4,
        out_specs=(vmem, vmem),
        scratch_shapes=[
            f32(*state.shape),
            f32(*surface.shape),
            pltpu.VMEM(surface.shape, jnp.int32),
            f32(16, 128),
            f32(64, 128),
            pltpu.SMEM((1, 4), jnp.int32),
            pltpu.SemaphoreType.DMA((4,)),
            f32(10, ROWS, 128),
            f32(10, ROWS, 128),
            f32(ROWS, 128),
            f32(ROWS, 128),
            f32(4, 32, 128),
            f32(2, 2, 32, 128),
            f32(SUB, 32, 128),
            f32(SUB, 32, 128),
            f32(5, 8, 128),
            f32(3, 80, 128),
            f32(4, 80, 128),
            f32(ROWS, 128),
            f32(ROWS, 128),
            pltpu.SemaphoreType.DMA((4,)),
            pltpu.SemaphoreType.DMA((4,)),
        ],
        compiler_params=pltpu.CompilerParams(
            collective_id=0, has_side_effects=True, vmem_limit_bytes=32 * 1024 * 1024
        ),
    )(*(pltpu.with_memory_space_constraint(x, pltpu.HBM) for x in (neighbours, state, surface, land_mask)))
    return new_state.reshape(state.shape), new_surface


def solution(mesh):
    spec = P(("tiles", "sub"))
    return jax.shard_map(
        functools.partial(shards, mesh.shape["tiles"]),
        mesh=mesh,
        in_specs=(spec, spec, spec, spec),
        out_specs=(spec, spec),
        check_vma=False,
    )
```

```python
import functools

import jax
import jax.numpy as jnp
from jax import lax
from jax.experimental import pallas as pl
from jax.experimental.pallas import tpu as pltpu
from jax.sharding import PartitionSpec as P

MESH = pl.DeviceIdType.MESH
TILE = 60
STEPS = 2
SUBCYCLES = 4
SUB = 8

time_step = 0.2
mixing = 0.02
coriolis = 0.5
gravity_step = 0.25
depth_step = 0.25

TOP = 24
ROWS = 112
ETA, WET = 8, 9
ITEMS = (
    [(4 + i, 17 * i, 17) for i in range(4)]
    + [(ETA, 68, 16), (WET, 84, 16)]
    + [(i, 100 + 4 * i, 4) for i in range(4)]
)
HALVES = (0, 28)
LISTED = 116


def lanes(shape):
    return lax.broadcasted_iota(jnp.int32, shape, len(shape) - 1)


def turn(x, shift):
    shift %= 128
    return pltpu.roll(x, shift, x.ndim - 1) if shift else x


def within(lane, first, count):
    return (lane >= first) & (lane < first + count)


def spread(tile_of, last, write):
    lane = lanes((8, 128))
    for b in range(8):
        row = 8 * b + lax.broadcasted_iota(jnp.int32, (8, 128), 0)
        begin = TILE * row
        tile = (begin + ((lane - begin) & 127)) >> 7
        first = (480 * b) // 128
        flat = jnp.zeros((8, 128), jnp.float32)
        for a in range(first, min((480 * b + 479) // 128, 28) + 1):
            flat = jnp.where(tile == a, jnp.broadcast_to(last if a == 28 else tile_of(a), (8, 128)), flat)
        flat = jnp.where(row & 1 == 1, turn(flat, 64), flat)
        rows = pltpu.roll(flat, (-480 * b) % 128, 1, stride=4, stride_axis=0)
        count = min(8, TILE - 8 * b)
        write(8 * b, count, jnp.where(lane < TILE, rows, 0.0)[0:count])


def flatten(rows, b):
    row = lax.broadcasted_iota(jnp.int32, (8, 128), 0)
    rows = jnp.where(row & 1 == 1, turn(rows, 480 * b + 60), turn(rows, 480 * b))
    rows = jnp.where(row & 2 == 2, turn(rows, 120), rows)
    return jnp.where(row & 4 == 4, turn(rows, 240), rows)


def joined(row_of, a, height):
    lane = lanes((height, 128)) + 128 * a
    first = (128 * a) // TILE
    out = row_of(first)
    for i in range(first + 1, min((128 * a + 127) // TILE, TILE - 1) + 1):
        out = jnp.where(lane < TILE * i, out, row_of(i))
    return out


def pack_side(D, side, at, mine):
    lane = lanes((TILE, 128))
    strip = jnp.zeros((TILE, 128), jnp.float32)
    for item, first, depth in ITEMS:
        whole = D[item, TOP : TOP + TILE]
        strip = jnp.where(within(lane, first, depth), turn(whole, first - at * (TILE - depth)), strip)
    for half, row in enumerate(HALVES):
        side[half] = strip[row : row + 32]
        side[half, 0:1] += mine


def pack_ends(D, ns, mine):
    def both(item, north, south, count):
        return D[item, TOP + north : TOP + north + count] + turn(D[item, TOP + south : TOP + south + count], 64)

    for i in range(4):
        ns[i] = both(4 + i, 0, 43, 16)
        ns[6, 4 * i : 4 * i + 4] = both(i, 0, 56, 4)
        ns[7, i : i + 1] = both(4 + i, 16, 59, 1)
    ns[4] = both(ETA, 0, 44, 16)
    ns[5] = both(WET, 0, 44, 16)
    ns[7, 4:16] = jnp.zeros((12, 128), jnp.float32)
    for m in range(SUB):
        ns[m, 0:1] += mine


def take(table, index):
    out = jnp.full((SUB, 128), -1.0, jnp.float32)
    for k in range(SUB):
        out = jnp.where(index == k, jnp.broadcast_to(table[k : k + 1], (SUB, 128)), out)
    return out


def table(held):
    return jnp.concatenate([held[r, 0:1] for r in range(SUB)], 0)


def column_of(rows, lane):
    return jnp.broadcast_to(rows[:, lane : lane + 1], (SUB, 128))


def wanted(own_in, me, lists):
    own = table(own_in)
    north, east, south, west = (column_of(own, TILE + direction) for direction in range(4))
    beside = jnp.where(lax.rem(me, 2) == 0, east, west)
    lists[0] = jnp.where(lanes((SUB, 128)) < 64, south, north)
    lists[1] = beside
    beyond = jnp.where(lax.rem(me, 4) >= 2, north, south)
    lists[3] = beyond
    lists[4] = take(beside, beyond)


def corners(side_in, me, lists):
    side = table(side_in)
    around = jnp.where(lax.rem(me, 4) >= 2, column_of(side, LISTED), column_of(side, LISTED + 2))
    lists[2] = jnp.where(lists[3] >= 0, lists[4], take(around, lists[1]))


def unpack_ends(D, got):
    def put(item, rows, north, south):
        count = rows.shape[0]
        tile = lanes((count, 128)) < TILE
        D[item, TOP + north : TOP + north + count] = jnp.where(tile, turn(rows, 64), 0.0)
        D[item, TOP + south : TOP + south + count] = jnp.where(tile, rows, 0.0)

    for i in range(4):
        put(4 + i, got[i], -17, 60)
        put(4 + i, got[7, i : i + 1], -1, 76)
        put(i, got[6, 4 * i : 4 * i + 4], -4, 60)
    put(ETA, got[4], -16, 60)
    put(WET, got[5], -16, 60)


def unpack_sides(D, got, eb, wb):
    for held, odd in ((eb, 0), (wb, 1)):
        held[8:24] = got[2 + odd, 32:48]
        for half, row in enumerate(HALVES):
            held[TOP + row : TOP + row + 32] = got[2 * half + odd, 0:32]
        held[84:100] = got[odd, 32:48]

    for item, first, depth in ITEMS:
        beyond = min(depth, 16)
        begin, count = TOP - beyond, TILE + 2 * beyond
        lane = lanes((count, 128))
        east = turn(eb[begin : begin + count], TILE - first)
        west = turn(wb[begin : begin + count], 128 - depth - first)
        sides = jnp.where(within(lane, TILE, depth), east, jnp.where(lane >= 128 - depth, west, 0.0))
        D[item, begin : begin + count] = D[item, begin : begin + count] + sides


def clinic(D, N, wets, field, begin, count):
    def at(which, shift=0):
        return D[2 * which : 2 * which + 2, begin + shift : begin + shift + count]

    mid, north, south = at(field), at(field, -1), at(field, 1)
    half_u = (0.5 * time_step) * at(2)
    half_v = (0.5 * time_step) * at(3)
    right, left = turn(mid, -1), turn(mid, 1)
    pair = north + south
    cross = 2.0 * pair - 8.0 * mid
    far = (at(field, -2) + at(field, 2)) + (turn(cross + right, -1) + turn(cross + left, 1))
    rate = time_step * mixing
    new = (1.0 - 20.0 * rate) * mid + (8.0 * rate) * pair - rate * far
    new = new - half_u * (right - left) - half_v * (south - north)
    if field == 2:
        new = new + (2.0 * coriolis) * half_v
    if field == 3:
        new = new - (2.0 * coriolis) * half_u
    N[2 * field : 2 * field + 2, begin : begin + count] = new * wets[begin : begin + count][None]


def vertices(D, N, wets):
    rate = time_step * mixing
    lane = lanes((8, 2, 128))
    for row in (TOP - 1, TOP + TILE - 1):
        swapped = jnp.concatenate([D[0:8, row + 1 : row + 2], D[0:8, row : row + 1]], 1)
        diagonal = jnp.where(
            (lane == 0) | (lane == TILE),
            turn(swapped, 1),
            jnp.where((lane == 127) | (lane == TILE - 1), turn(swapped, -1), 0.0),
        )
        N[0:8, row : row + 2] += (2.0 * rate) * diagonal * wets[row : row + 2][None]


def tropic(heights, norths, wet_at, eta, zonal, meridional, begin, count):
    for _ in range(SUBCYCLES):
        heights[begin : begin + count] = eta
        norths[begin : begin + count] = meridional

        def a(shift):
            return heights[begin + shift : begin + shift + count]

        def c(shift):
            return norths[begin + shift : begin + shift + count]

        new_u = zonal - (gravity_step * 0.5) * (turn(eta, -1) - turn(eta, 1))
        new_v = meridional - (gravity_step * 0.5) * (a(1) - a(-1))
        along = (c(1) - c(-1)) - (gravity_step * 0.5) * ((a(2) - eta) - (eta - a(-2)))
        spread = (turn(new_u, -1) - turn(new_u, 1)) + along
        wet = wet_at(begin, count)
        eta = (eta - (depth_step * 0.5) * spread) * wet
        zonal, meridional = new_u * wet, new_v * wet
    return eta, zonal, meridional


def kernel(
    columns,
    near_in,
    state_in,
    surface_in,
    mask_in,
    new_state,
    new_surface,
    state,
    surface,
    mask,
    tails,
    turned,
    near,
    loaded,
    D,
    N,
    heights,
    norths,
    ns,
    sides,
    own_in,
    side_in,
    lists,
    out_ends,
    got_ends,
    out,
    got,
    eb,
    wb,
    sent,
    came,
):
    column, me = lax.axis_index("tiles"), lax.axis_index("sub")
    quarter, odd = lax.rem(me, 4), lax.rem(me, 2)
    after, before = lax.rem(column + 1, columns), lax.rem(column + columns - 1, columns)
    source = lax.rem(column + columns + 1 - 2 * odd, columns)
    others = [lax.rem(me + k, SUB) for k in (4, 3, 5, 2, 6, 1, 7)]
    pairs = [lax.rem(me // 2 + k, 4) for k in (2, 1, 3, 0)]
    turns = 1 - 2 * lax.rem(column, 2)
    close = [lax.rem(me + SUB + turns * k, SUB) for k in (2, 1, -1)]

    loads = [
        pltpu.make_async_copy(held, target, loaded.at[i])
        for i, (held, target) in enumerate(((mask_in, mask), (surface_in, surface), (state_in, state), (near_in, near)))
    ]
    for load in loads:
        load.start()

    barrier = pltpu.get_barrier_semaphore()
    for k in (4, 3, 5, 2, 6, 1, 7, 0):
        r = lax.rem(me + k, SUB)
        pl.semaphore_signal(barrier, inc=1, device_id=(source, r), device_id_type=MESH)
        if k:
            pl.semaphore_signal(barrier, inc=1, device_id=(column, r), device_id_type=MESH)

    D[...] = jnp.zeros_like(D)

    def put(item):
        def write(at, count, rows):
            if item != WET:
                rows = rows * D[WET, TOP + at : TOP + at + count]
            D[item, TOP + at : TOP + at + count] = rows

        return write

    loads[0].wait()
    tails[0:1, 0:16] = mask[0:1, 3584:3600].astype(jnp.float32)
    spread(lambda a: mask[0:1, 128 * a : 128 * a + 128].astype(jnp.float32), tails[0:1], put(WET))
    loads[1].wait()
    tails[1:2, 0:16] = surface[0:1, 3584:3600]
    spread(lambda a: surface[0:1, 128 * a : 128 * a + 128], tails[1:2], put(ETA))
    loads[2].wait()
    for field in range(4):
        tails[8 + 2 * field : 10 + 2 * field, 0:16] = state[0, field, :, 3584:3600]
        for level in range(2):
            item = 2 * field + level
            spread(
                lambda a, field=field, level=level: state[0, field, level : level + 1, 128 * a : 128 * a + 128],
                tails[8 + item : 9 + item],
                put(item),
            )
    loads[3].wait()
    lane = lanes((1, 128))
    mine = jnp.zeros((1, 128), jnp.float32)
    for direction, base in enumerate((column, column + 1, column, column - 1)):
        listed = near[0, direction]
        slot = jnp.where(listed >= 0, listed - base * SUB, -1).astype(jnp.float32)
        mine = jnp.where(lane == TILE + direction, slot, mine)

    def send(source_ref, target, kind, device):
        pltpu.make_async_remote_copy(
            src_ref=source_ref,
            dst_ref=target,
            send_sem=sent.at[kind],
            recv_sem=came.at[kind],
            device_id=device,
            device_id_type=MESH,
        ).start()

    def wait(ref, semaphore):
        pltpu.make_async_copy(ref, ref, semaphore).wait()

    pack_side(D, sides.at[0], 1, turn(mine, LISTED - TILE))
    pl.semaphore_wait(barrier, 15)
    for pair in pairs:
        send(sides.at[0, lax.rem(pair, 2)], side_in.at[me], 1, (after, 2 * pair + 1))
    pack_side(D, sides.at[1], 0, turn(mine, LISTED - TILE))
    for pair in pairs:
        send(sides.at[1, lax.rem(pair, 2)], side_in.at[me], 1, (before, 2 * pair))
    pack_ends(D, ns, mine)
    own_in[me] = ns[me]
    for r in others:
        send(ns.at[r], own_in.at[me], 0, (column, r))

    N[...] = jnp.zeros_like(N)
    heights[...] = jnp.zeros_like(heights)
    norths[...] = jnp.zeros_like(norths)

    def fill(target, slot, r, which, held, begin, at, count):
        want = jnp.broadcast_to(lists[which, pl.ds(r, 1)], (8, 128))
        parts = [jnp.zeros((8, 128), jnp.float32)] * (count // 8)
        for k in range(SUB):
            hit = want == k
            for i in range(count // 8):
                parts[i] = jnp.where(hit, held[k, pl.ds(begin + 8 * i, 8)], parts[i])
        for i, part in enumerate(parts):
            target[slot, at + 8 * i : at + 8 * i + 8] = part

    def fill_sides(target, slot, r):
        fill(target, slot, r, 1, side_in, 0, 0, 32)
        fill(target, slot, r, 2, side_in, pl.multiple_of(16 * (quarter // 2), 16), 32, 16)

    seven, eight, three = pl.ds(0, SUB - 1), pl.ds(0, SUB), pl.ds(0, 3)
    wait(own_in.at[seven], came.at[0])
    wanted(own_in, me, lists)
    for r in others:
        fill(out_ends, r, r, 0, own_in, 0, 0, 16)
        send(out_ends.at[r], got_ends.at[me], 2, (column, r))
    fill(got_ends, me, me, 0, own_in, 0, 0, 16)

    wait(side_in.at[eight], came.at[1])
    corners(side_in, me, lists)
    for i, r in enumerate(close):
        fill_sides(out, i, r)
        send(out.at[i], got.at[quarter], 3, (column, r))
    fill_sides(got, quarter, me)

    wait(got_ends.at[seven], came.at[2])
    unpack_ends(D, got_ends)
    wait(got.at[three], came.at[3])
    unpack_sides(D, got, eb, wb)
    weights = (2.0 / 6.0, 4.0 / 6.0)
    fields, other = D, N
    wet_at = lambda begin, count: D[WET, begin : begin + count]
    for step in range(STEPS):
        begin, count = ((8, 96), (16, 80))[step]
        tracer = ((16, 72), (24, 64))[step]
        for field in (2, 3):
            clinic(fields, other, D.at[WET], field, begin, count)
        for field in (0, 1):
            clinic(fields, other, D.at[WET], field, *tracer)
        vertices(fields, other, D.at[WET])
        rows = slice(begin, begin + count)
        old_u = weights[0] * other[4, rows] + weights[1] * other[5, rows]
        old_v = weights[0] * other[6, rows] + weights[1] * other[7, rows]
        eta, zonal, meridional = tropic(heights, norths, wet_at, fields[ETA, rows], old_u, old_v, begin, count)
        other[ETA, rows] = eta
        for level in range(2):
            other[4 + level, rows] += zonal - old_u
            other[6 + level, rows] += meridional - old_v
        fields, other = other, fields

    for item in range(8):
        new_state[item] = fields[item, TOP : TOP + TILE, 0:TILE]
    for b in range(8):
        turned[8 * b : 8 * b + 8] = flatten(fields[ETA, TOP + 8 * b : TOP + 8 * b + 8], b)
    for a in range(29):
        width = min(128, TILE * TILE - 128 * a)
        tile = joined(lambda i: turned[i : i + 1], a, 1)
        new_surface[0:1, 128 * a : 128 * a + width] = tile[:, 0:width]

    wait(own_in.at[seven], sent.at[0])
    wait(side_in.at[eight], sent.at[1])
    wait(got_ends.at[seven], sent.at[2])
    wait(got.at[three], sent.at[3])


def shards(columns, state, surface, land_mask, neighbours):
    hbm, vmem = pl.BlockSpec(memory_space=pltpu.HBM), pl.BlockSpec(memory_space=pltpu.VMEM)
    f32 = lambda *shape: pltpu.VMEM(shape, jnp.float32)
    new_state, new_surface = pl.pallas_call(
        functools.partial(kernel, columns),
        out_shape=(
            jax.ShapeDtypeStruct((8, TILE, TILE), jnp.float32),
            jax.ShapeDtypeStruct(surface.shape, jnp.float32),
        ),
        in_specs=[hbm] * 4,
        out_specs=(vmem, vmem),
        scratch_shapes=[
            f32(*state.shape),
            f32(*surface.shape),
            pltpu.VMEM(surface.shape, jnp.int32),
            f32(16, 128),
            f32(64, 128),
            pltpu.SMEM((1, 4), jnp.int32),
            pltpu.SemaphoreType.DMA((4,)),
            f32(10, ROWS, 128),
            f32(10, ROWS, 128),
            f32(ROWS, 128),
            f32(ROWS, 128),
            f32(SUB, 16, 128),
            f32(2, 2, 32, 128),
            f32(SUB, 16, 128),
            f32(SUB, 32, 128),
            f32(5, 8, 128),
            f32(SUB, 16, 128),
            f32(SUB, 16, 128),
            f32(3, 48, 128),
            f32(4, 48, 128),
            f32(ROWS, 128),
            f32(ROWS, 128),
            pltpu.SemaphoreType.DMA((4,)),
            pltpu.SemaphoreType.DMA((4,)),
        ],
        compiler_params=pltpu.CompilerParams(
            collective_id=0, has_side_effects=True, vmem_limit_bytes=32 * 1024 * 1024
        ),
    )(*(pltpu.with_memory_space_constraint(x, pltpu.HBM) for x in (neighbours, state, surface, land_mask)))
    return new_state.reshape(state.shape), new_surface


def solution(mesh):
    spec = P(("tiles", "sub"))
    return jax.shard_map(
        functools.partial(shards, mesh.shape["tiles"]),
        mesh=mesh,
        in_specs=(spec, spec, spec, spec),
        out_specs=(spec, spec),
        check_vma=False,
    )
```

```python
import functools

import jax
import jax.numpy as jnp
from jax import lax
from jax.experimental import pallas as pl
from jax.experimental.pallas import tpu as pltpu
from jax.sharding import PartitionSpec as P

MESH = pl.DeviceIdType.MESH
TILE = 60
STEPS = 2
SUBCYCLES = 4
SUB = 8

time_step = 0.2
mixing = 0.02
coriolis = 0.5
gravity_step = 0.25
depth_step = 0.25

TOP = 24
ROWS = 112
ETA, WET = 8, 9
ITEMS = (
    [(4 + i, 17 * i, 17) for i in range(4)]
    + [(ETA, 68, 16), (WET, 84, 16)]
    + [(i, 100 + 4 * i, 4) for i in range(4)]
)
HALVES = (0, 28)
LISTED = 116


def lanes(shape):
    return lax.broadcasted_iota(jnp.int32, shape, len(shape) - 1)


def turn(x, shift):
    shift %= 128
    return pltpu.roll(x, shift, x.ndim - 1) if shift else x


def within(lane, first, count):
    return (lane >= first) & (lane < first + count)


def spread(tile_of, last, write):
    lane = lanes((8, 128))
    for b in range(8):
        row = 8 * b + lax.broadcasted_iota(jnp.int32, (8, 128), 0)
        begin = TILE * row
        tile = (begin + ((lane - begin) & 127)) >> 7
        first = (480 * b) // 128
        flat = jnp.zeros((8, 128), jnp.float32)
        for a in range(first, min((480 * b + 479) // 128, 28) + 1):
            flat = jnp.where(tile == a, jnp.broadcast_to(last if a == 28 else tile_of(a), (8, 128)), flat)
        flat = jnp.where(row & 1 == 1, turn(flat, 64), flat)
        rows = pltpu.roll(flat, (-480 * b) % 128, 1, stride=4, stride_axis=0)
        count = min(8, TILE - 8 * b)
        write(8 * b, count, jnp.where(lane < TILE, rows, 0.0)[0:count])


def flatten(rows, b):
    row = lax.broadcasted_iota(jnp.int32, (8, 128), 0)
    rows = jnp.where(row & 1 == 1, turn(rows, 480 * b + 60), turn(rows, 480 * b))
    rows = jnp.where(row & 2 == 2, turn(rows, 120), rows)
    return jnp.where(row & 4 == 4, turn(rows, 240), rows)


def joined(row_of, a, height):
    lane = lanes((height, 128)) + 128 * a
    first = (128 * a) // TILE
    out = row_of(first)
    for i in range(first + 1, min((128 * a + 127) // TILE, TILE - 1) + 1):
        out = jnp.where(lane < TILE * i, out, row_of(i))
    return out


def pack_side(D, side, at, mine):
    lane = lanes((TILE, 128))
    strip = jnp.zeros((TILE, 128), jnp.float32)
    for item, first, depth in ITEMS:
        whole = D[item, TOP : TOP + TILE]
        strip = jnp.where(within(lane, first, depth), turn(whole, first - at * (TILE - depth)), strip)
    for half, row in enumerate(HALVES):
        side[half] = strip[row : row + 32]
        side[half, 0:1] += mine


def pack_ends(D, ns, mine):
    def both(item, north, south, count):
        return D[item, TOP + north : TOP + north + count] + turn(D[item, TOP + south : TOP + south + count], 64)

    for i in range(4):
        ns[i] = both(4 + i, 0, 43, 16)
        ns[6, 4 * i : 4 * i + 4] = both(i, 0, 56, 4)
        ns[7, i : i + 1] = both(4 + i, 16, 59, 1)
    ns[4] = both(ETA, 0, 44, 16)
    ns[5] = both(WET, 0, 44, 16)
    ns[7, 4:16] = jnp.zeros((12, 128), jnp.float32)
    for m in range(SUB):
        ns[m, 0:1] += mine


def take(table, index):
    out = jnp.full((SUB, 128), -1.0, jnp.float32)
    for k in range(SUB):
        out = jnp.where(index == k, jnp.broadcast_to(table[k : k + 1], (SUB, 128)), out)
    return out


def table(held):
    return jnp.concatenate([held[r, 0:1] for r in range(SUB)], 0)


def column_of(rows, lane):
    return jnp.broadcast_to(rows[:, lane : lane + 1], (SUB, 128))


def wanted(own_in, me, lists):
    own = table(own_in)
    north, east, south, west = (column_of(own, TILE + direction) for direction in range(4))
    beside = jnp.where(lax.rem(me, 2) == 0, east, west)
    lists[0] = jnp.where(lanes((SUB, 128)) < 64, south, north)
    lists[1] = beside
    beyond = jnp.where(lax.rem(me, 4) >= 2, north, south)
    lists[3] = beyond
    lists[4] = take(beside, beyond)


def corners(side_in, me, lists):
    side = table(side_in)
    around = jnp.where(lax.rem(me, 4) >= 2, column_of(side, LISTED), column_of(side, LISTED + 2))
    lists[2] = jnp.where(lists[3] >= 0, lists[4], take(around, lists[1]))


def unpack_ends(D, got):
    def put(item, rows, north, south):
        count = rows.shape[0]
        tile = lanes((count, 128)) < TILE
        D[item, TOP + north : TOP + north + count] = jnp.where(tile, turn(rows, 64), 0.0)
        D[item, TOP + south : TOP + south + count] = jnp.where(tile, rows, 0.0)

    for i in range(4):
        put(4 + i, got[i], -17, 60)
        put(4 + i, got[7, i : i + 1], -1, 76)
        put(i, got[6, 4 * i : 4 * i + 4], -4, 60)
    put(ETA, got[4], -16, 60)
    put(WET, got[5], -16, 60)


def unpack_sides(D, got, eb, wb):
    for held, odd in ((eb, 0), (wb, 1)):
        held[8:24] = got[2 + odd, 32:48]
        for half, row in enumerate(HALVES):
            held[TOP + row : TOP + row + 32] = got[2 * half + odd, 0:32]
        held[84:100] = got[odd, 32:48]

    for item, first, depth in ITEMS:
        beyond = min(depth, 16)
        begin, count = TOP - beyond, TILE + 2 * beyond
        lane = lanes((count, 128))
        east = turn(eb[begin : begin + count], TILE - first)
        west = turn(wb[begin : begin + count], 128 - depth - first)
        sides = jnp.where(within(lane, TILE, depth), east, jnp.where(lane >= 128 - depth, west, 0.0))
        D[item, begin : begin + count] = D[item, begin : begin + count] + sides


def clinic(D, N, wets, field, begin, count):
    def at(which, shift=0):
        return D[2 * which : 2 * which + 2, begin + shift : begin + shift + count]

    mid, north, south = at(field), at(field, -1), at(field, 1)
    half_u = (0.5 * time_step) * at(2)
    half_v = (0.5 * time_step) * at(3)
    right, left = turn(mid, -1), turn(mid, 1)
    pair = north + south
    cross = 2.0 * pair - 8.0 * mid
    far = (at(field, -2) + at(field, 2)) + (turn(cross + right, -1) + turn(cross + left, 1))
    rate = time_step * mixing
    new = (1.0 - 20.0 * rate) * mid + (8.0 * rate) * pair - rate * far
    new = new - half_u * (right - left) - half_v * (south - north)
    if field == 2:
        new = new + (2.0 * coriolis) * half_v
    if field == 3:
        new = new - (2.0 * coriolis) * half_u
    N[2 * field : 2 * field + 2, begin : begin + count] = new * wets[begin : begin + count][None]


def vertices(D, N, wets):
    rate = time_step * mixing
    lane = lanes((8, 2, 128))
    for row in (TOP - 1, TOP + TILE - 1):
        swapped = jnp.concatenate([D[0:8, row + 1 : row + 2], D[0:8, row : row + 1]], 1)
        diagonal = jnp.where(
            (lane == 0) | (lane == TILE),
            turn(swapped, 1),
            jnp.where((lane == 127) | (lane == TILE - 1), turn(swapped, -1), 0.0),
        )
        N[0:8, row : row + 2] += (2.0 * rate) * diagonal * wets[row : row + 2][None]


def tropic(heights, norths, wet_at, eta, zonal, meridional, begin, count):
    for _ in range(SUBCYCLES):
        heights[begin : begin + count] = eta
        norths[begin : begin + count] = meridional

        def a(shift):
            return heights[begin + shift : begin + shift + count]

        def c(shift):
            return norths[begin + shift : begin + shift + count]

        pull = gravity_step * 0.5
        new_u = zonal - pull * (turn(eta, -1) - turn(eta, 1))
        new_v = meridional - pull * (a(1) - a(-1))
        across = (turn(zonal, -1) - turn(zonal, 1)) + (c(1) - c(-1))
        spread = across - pull * ((turn(eta, -2) + turn(eta, 2)) + (a(2) + a(-2)) - 4.0 * eta)
        wet = wet_at(begin, count)
        eta = (eta - (depth_step * 0.5) * spread) * wet
        zonal, meridional = new_u * wet, new_v * wet
    return eta, zonal, meridional


def kernel(
    columns,
    near_in,
    state_in,
    surface_in,
    mask_in,
    new_state,
    new_surface,
    state,
    surface,
    mask,
    tails,
    turned,
    near,
    loaded,
    D,
    N,
    heights,
    norths,
    ns,
    sides,
    own_in,
    side_in,
    lists,
    out_ends,
    got_ends,
    out,
    got,
    eb,
    wb,
    sent,
    came,
):
    column, me = lax.axis_index("tiles"), lax.axis_index("sub")
    quarter, odd = lax.rem(me, 4), lax.rem(me, 2)
    after, before = lax.rem(column + 1, columns), lax.rem(column + columns - 1, columns)
    source = lax.rem(column + columns + 1 - 2 * odd, columns)
    others = [lax.rem(me + k, SUB) for k in (4, 3, 5, 2, 6, 1, 7)]
    pairs = [lax.rem(me // 2 + k, 4) for k in (2, 1, 3, 0)]
    turns = 1 - 2 * lax.rem(column, 2)
    close = [lax.rem(me + SUB + turns * k, SUB) for k in (2, 1, -1)]

    loads = [
        pltpu.make_async_copy(held, target, loaded.at[i])
        for i, (held, target) in enumerate(((mask_in, mask), (surface_in, surface), (state_in, state), (near_in, near)))
    ]
    for load in loads:
        load.start()

    barrier = pltpu.get_barrier_semaphore()
    for k in (4, 3, 5, 2, 6, 1, 7, 0):
        r = lax.rem(me + k, SUB)
        pl.semaphore_signal(barrier, inc=1, device_id=(source, r), device_id_type=MESH)
        if k:
            pl.semaphore_signal(barrier, inc=1, device_id=(column, r), device_id_type=MESH)

    D[...] = jnp.zeros_like(D)

    def put(item):
        def write(at, count, rows):
            if item != WET:
                rows = rows * D[WET, TOP + at : TOP + at + count]
            D[item, TOP + at : TOP + at + count] = rows

        return write

    loads[0].wait()
    tails[0:1, 0:16] = mask[0:1, 3584:3600].astype(jnp.float32)
    spread(lambda a: mask[0:1, 128 * a : 128 * a + 128].astype(jnp.float32), tails[0:1], put(WET))
    loads[1].wait()
    tails[1:2, 0:16] = surface[0:1, 3584:3600]
    spread(lambda a: surface[0:1, 128 * a : 128 * a + 128], tails[1:2], put(ETA))
    loads[2].wait()
    for field in range(4):
        tails[8 + 2 * field : 10 + 2 * field, 0:16] = state[0, field, :, 3584:3600]
        for level in range(2):
            item = 2 * field + level
            spread(
                lambda a, field=field, level=level: state[0, field, level : level + 1, 128 * a : 128 * a + 128],
                tails[8 + item : 9 + item],
                put(item),
            )
    loads[3].wait()
    lane = lanes((1, 128))
    mine = jnp.zeros((1, 128), jnp.float32)
    for direction, base in enumerate((column, column + 1, column, column - 1)):
        listed = near[0, direction]
        slot = jnp.where(listed >= 0, listed - base * SUB, -1).astype(jnp.float32)
        mine = jnp.where(lane == TILE + direction, slot, mine)

    def send(source_ref, target, kind, device):
        pltpu.make_async_remote_copy(
            src_ref=source_ref,
            dst_ref=target,
            send_sem=sent.at[kind],
            recv_sem=came.at[kind],
            device_id=device,
            device_id_type=MESH,
        ).start()

    def wait(ref, semaphore):
        pltpu.make_async_copy(ref, ref, semaphore).wait()

    pack_side(D, sides.at[0], 1, turn(mine, LISTED - TILE))
    pl.semaphore_wait(barrier, 15)
    for pair in pairs:
        send(sides.at[0, lax.rem(pair, 2)], side_in.at[me], 1, (after, 2 * pair + 1))
    pack_side(D, sides.at[1], 0, turn(mine, LISTED - TILE))
    for pair in pairs:
        send(sides.at[1, lax.rem(pair, 2)], side_in.at[me], 1, (before, 2 * pair))
    pack_ends(D, ns, mine)
    own_in[me] = ns[me]
    for r in others:
        send(ns.at[r], own_in.at[me], 0, (column, r))

    N[...] = jnp.zeros_like(N)
    heights[...] = jnp.zeros_like(heights)
    norths[...] = jnp.zeros_like(norths)

    def fill(target, slot, r, which, held, begin, at, count):
        want = jnp.broadcast_to(lists[which, pl.ds(r, 1)], (8, 128))
        parts = [jnp.zeros((8, 128), jnp.float32)] * (count // 8)
        for k in range(SUB):
            hit = want == k
            for i in range(count // 8):
                parts[i] = jnp.where(hit, held[k, pl.ds(begin + 8 * i, 8)], parts[i])
        for i, part in enumerate(parts):
            target[slot, at + 8 * i : at + 8 * i + 8] = part

    def fill_sides(target, slot, r):
        fill(target, slot, r, 1, side_in, 0, 0, 32)
        fill(target, slot, r, 2, side_in, pl.multiple_of(16 * (quarter // 2), 16), 32, 16)

    seven, eight, three = pl.ds(0, SUB - 1), pl.ds(0, SUB), pl.ds(0, 3)
    wait(own_in.at[seven], came.at[0])
    wanted(own_in, me, lists)
    for r in others:
        fill(out_ends, r, r, 0, own_in, 0, 0, 16)
        send(out_ends.at[r], got_ends.at[me], 2, (column, r))
    fill(got_ends, me, me, 0, own_in, 0, 0, 16)

    wait(side_in.at[eight], came.at[1])
    corners(side_in, me, lists)
    for i, r in enumerate(close):
        fill_sides(out, i, r)
        send(out.at[i], got.at[quarter], 3, (column, r))
    fill_sides(got, quarter, me)

    wait(got_ends.at[seven], came.at[2])
    unpack_ends(D, got_ends)
    wait(got.at[three], came.at[3])
    unpack_sides(D, got, eb, wb)
    weights = (2.0 / 6.0, 4.0 / 6.0)
    fields, other = D, N
    wet_at = lambda begin, count: D[WET, begin : begin + count]
    for step in range(STEPS):
        begin, count = ((8, 96), (16, 80))[step]
        tracer = ((16, 72), (24, 64))[step]
        for field in (2, 3):
            clinic(fields, other, D.at[WET], field, begin, count)
        for field in (0, 1):
            clinic(fields, other, D.at[WET], field, *tracer)
        vertices(fields, other, D.at[WET])
        rows = slice(begin, begin + count)
        old_u = weights[0] * other[4, rows] + weights[1] * other[5, rows]
        old_v = weights[0] * other[6, rows] + weights[1] * other[7, rows]
        eta, zonal, meridional = tropic(heights, norths, wet_at, fields[ETA, rows], old_u, old_v, begin, count)
        other[ETA, rows] = eta
        for level in range(2):
            other[4 + level, rows] += zonal - old_u
            other[6 + level, rows] += meridional - old_v
        fields, other = other, fields

    for item in range(8):
        new_state[item] = fields[item, TOP : TOP + TILE, 0:TILE]
    for b in range(8):
        turned[8 * b : 8 * b + 8] = flatten(fields[ETA, TOP + 8 * b : TOP + 8 * b + 8], b)
    for a in range(29):
        width = min(128, TILE * TILE - 128 * a)
        tile = joined(lambda i: turned[i : i + 1], a, 1)
        new_surface[0:1, 128 * a : 128 * a + width] = tile[:, 0:width]

    wait(own_in.at[seven], sent.at[0])
    wait(side_in.at[eight], sent.at[1])
    wait(got_ends.at[seven], sent.at[2])
    wait(got.at[three], sent.at[3])


def shards(columns, state, surface, land_mask, neighbours):
    hbm, vmem = pl.BlockSpec(memory_space=pltpu.HBM), pl.BlockSpec(memory_space=pltpu.VMEM)
    f32 = lambda *shape: pltpu.VMEM(shape, jnp.float32)
    new_state, new_surface = pl.pallas_call(
        functools.partial(kernel, columns),
        out_shape=(
            jax.ShapeDtypeStruct((8, TILE, TILE), jnp.float32),
            jax.ShapeDtypeStruct(surface.shape, jnp.float32),
        ),
        in_specs=[hbm] * 4,
        out_specs=(vmem, vmem),
        scratch_shapes=[
            f32(*state.shape),
            f32(*surface.shape),
            pltpu.VMEM(surface.shape, jnp.int32),
            f32(16, 128),
            f32(64, 128),
            pltpu.SMEM((1, 4), jnp.int32),
            pltpu.SemaphoreType.DMA((4,)),
            f32(10, ROWS, 128),
            f32(10, ROWS, 128),
            f32(ROWS, 128),
            f32(ROWS, 128),
            f32(SUB, 16, 128),
            f32(2, 2, 32, 128),
            f32(SUB, 16, 128),
            f32(SUB, 32, 128),
            f32(5, 8, 128),
            f32(SUB, 16, 128),
            f32(SUB, 16, 128),
            f32(3, 48, 128),
            f32(4, 48, 128),
            f32(ROWS, 128),
            f32(ROWS, 128),
            pltpu.SemaphoreType.DMA((4,)),
            pltpu.SemaphoreType.DMA((4,)),
        ],
        compiler_params=pltpu.CompilerParams(
            collective_id=0, has_side_effects=True, vmem_limit_bytes=32 * 1024 * 1024
        ),
    )(*(pltpu.with_memory_space_constraint(x, pltpu.HBM) for x in (neighbours, state, surface, land_mask)))
    return new_state.reshape(state.shape), new_surface


def solution(mesh):
    spec = P(("tiles", "sub"))
    return jax.shard_map(
        functools.partial(shards, mesh.shape["tiles"]),
        mesh=mesh,
        in_specs=(spec, spec, spec, spec),
        out_specs=(spec, spec),
        check_vma=False,
    )
```
